512 devices in a mesh: section: 2 (over core), row: 8 (over y), col: 32 (over x, z).
Axes of the slice: x: 4, y: 8, z: 8, core: 2. Of those that a mesh axis runs over, the one named last changes fastest.
Arguments:
- x_stash: bfloat16 [2, 1, 128, 16384], P('section', None, 'col', 'row'), may hold values from -6 to 6
- out_grad: bfloat16 [1, 128, 16384], P(None, 'col', 'row'), may hold values from -6 to 6
- in_values: bfloat16 [2, 8, 32, 64, 64, 128], P('section', 'row', 'col'), as said below
- in_index: int32 [2, 8, 32, 2, 128], P('section', 'row', 'col'), may hold values from 0 to 31, as said below
- out_values: bfloat16 [2, 8, 32, 64, 64, 128], P('section', 'row', 'col'), as said below
- out_index: int32 [2, 8, 32, 2, 128], P('section', 'row', 'col'), may hold values from 0 to 31, as said below
Outputs:
- in_grad: bfloat16 [2, 1, 128, 16384], P('section', None, 'col', 'row')
The draws below stay inside these ranges and needn't reach their ends.
Inputs may be any that keep to these rules, and one draw needn't show every extreme that they name: `in_index`: the slots of one tile name distinct blocks. Each tile holds between 32 and 128 nonzero blocks in its first slots, and its later slots of in_values (out_values) are zero; in every draw one tile of each layer's matrix fills all 128 slots, and which one is drawn. `out_index`: same law as in_index, drawn apart. `in_values`: slots past a tile's count of nonzero blocks are zero. `out_values`: slots past a tile's count of nonzero blocks are zero.
All inputs are finite; a program needn't handle non-finite values.
Results may differ from the reference program's by a relative error of at most 0.034.
Values may be sent and summed in bfloat16 or wider, within the bound.
No kernel may reach another device: no remote copies, remote signals or barrier semaphores. Data moves between devices by JAX's collectives and lax.ppermute only.
A program may use at most 64 MiB of HBM per device.

```python
import jax
import jax.numpy as jnp
from jax import lax

D = 16384
FF = 65536
BLK = 64
SLOTS = 128
MB_TOK = 128
MICRO = 1
N_ROW = 8
N_COL = 32


def slot_counts(key, marker):
    key = jax.random.fold_in(key, marker)
    first_key, second_key = jax.random.split(key)
    spread = jax.random.randint(first_key, (2, N_ROW * N_COL), 0, 1001)
    quarter = SLOTS // 4
    counts = quarter + (SLOTS - quarter) * spread * spread // 1000000
    busiest = jax.random.randint(second_key, (2,), 0, N_ROW * N_COL)
    counts = counts.at[jnp.arange(2), busiest].set(SLOTS)
    return counts.reshape(2, N_ROW, N_COL)


def block_scale():
    side_total = D // N_ROW // BLK * (FF // N_COL // BLK)
    return (2.0 * side_total / (SLOTS * D)) ** 0.5


def slot_positions(key):
    side_cols = FF // N_COL // BLK
    side_total = D // N_ROW // BLK * side_cols
    tile_keys = jax.random.split(key, 2 * N_ROW * N_COL)
    chosen = jax.vmap(lambda single: jax.random.permutation(single, side_total))(tile_keys)[:, :SLOTS]
    stacked = jnp.stack([chosen // side_cols, chosen % side_cols], axis=1)
    return stacked.reshape(2, N_ROW, N_COL, 2, SLOTS).astype(jnp.int32)


def live_slots(counts):
    return (jnp.arange(SLOTS)[None, None, None, :] < counts[..., None]).astype(jnp.float32)


def pair_slots(blocks):
    split = blocks.reshape(2, N_ROW, N_COL, SLOTS // 2, 2, BLK, BLK)
    moved = jnp.swapaxes(split, 4, 5)
    return moved.reshape(2, N_ROW, N_COL, SLOTS // 2, BLK, 2 * BLK)


def draw_in_values(key, part):
    counts = slot_counts(key, 11)
    key = jax.random.fold_in(key, 1)
    shape = (2, N_ROW, N_COL, SLOTS, BLK, BLK)
    raw = jax.random.normal(key, shape, jnp.float32)
    blocks = raw * live_slots(counts)[..., None, None] * block_scale()
    return pair_slots(blocks).astype(jnp.bfloat16)


def draw_in_index(key, part):
    key = jax.random.fold_in(key, 2)
    return slot_positions(key)


def draw_out_values(key, part):
    counts = slot_counts(key, 12)
    key = jax.random.fold_in(key, 3)
    shape = (2, N_ROW, N_COL, SLOTS, BLK, BLK)
    raw = jax.random.normal(key, shape, jnp.float32)
    blocks = raw * live_slots(counts)[..., None, None] * block_scale()
    return pair_slots(blocks).astype(jnp.bfloat16)


def draw_out_index(key, part):
    key = jax.random.fold_in(key, 4)
    return slot_positions(key)


def level_of(key, shape, shards, low, high):
    def one(dim, blocks):
        draws = jax.random.uniform(jax.random.fold_in(jax.random.fold_in(key, 6), dim), (blocks,), jnp.float32, low / len(shards), high / len(shards))
        return jnp.repeat(jnp.exp(draws), shape[dim] // blocks).reshape((-1,) + (1,) * (len(shape) - dim - 1))

    loudness = one(*shards[0])
    for cut in shards[1:]:
        loudness = loudness * one(*cut)
    return loudness


def gaussian(own_key, dims, width, limit, cuts=(), kind=jnp.bfloat16):
    result = width * jax.random.normal(own_key, dims, jnp.float32)
    if cuts:
        result = result * level_of(own_key, dims, cuts, -0.22, 0.18)
    return jnp.clip(result, -limit, limit).astype(kind)


def setup_inputs(seed: int = 0) -> dict:
    streams_of = jax.random.split(jax.random.key(seed), 7)
    x_stash = gaussian(streams_of[0], (2, MICRO, MB_TOK, D), 1.0, 6.0, ((0, 2), (2, 32), (3, 8)))
    out_grad = gaussian(streams_of[1], (MICRO, MB_TOK, D), 1.0, 6.0, ((1, 32), (2, 8)))
    in_values = draw_in_values(jax.random.fold_in(streams_of[6], 71), 0)
    in_index = draw_in_index(jax.random.fold_in(streams_of[6], 71), 0)
    out_values = draw_out_values(jax.random.fold_in(streams_of[6], 71), 0)
    out_index = draw_out_index(jax.random.fold_in(streams_of[6], 71), 0)
    return dict(x_stash=x_stash, out_grad=out_grad, in_values=in_values, in_index=in_index, out_values=out_values, out_index=out_index)


forward_form = 'tnk,nkj->tnj'
backward_form = 'tnj,nkj->tnk'

def unpair(values):
    lead = values.shape[:-3]
    pairs = values.shape[-3]
    block_size = values.shape[-2]
    split = values.reshape(lead + (pairs, block_size, 2, block_size))
    moved = jnp.swapaxes(split, -3, -2)
    return moved.reshape(lead + (pairs * 2, block_size, block_size))

def tile_product(operand, values, source, target, blocks_out, pattern):
    block_size = values.shape[-1]
    picked = operand.reshape(operand.shape[0], -1, block_size)[:, source]
    products = jnp.einsum(pattern, picked.astype(jnp.float32), values.astype(jnp.float32), precision=lax.Precision.HIGHEST)
    summed = jnp.zeros((operand.shape[0], blocks_out, block_size), products.dtype).at[:, target].add(products)
    return summed.reshape(operand.shape[0], blocks_out * block_size)

def gelu_slope(hidden):
    return 0.5 * (1.0 + lax.erf(hidden * 0.7071067811865476)) + hidden * jnp.exp(-0.5 * hidden * hidden) * 0.3989422804014327

def layer_grad(stash_now, upstream, in_values, in_index, out_values, out_index):
    rows_tile = D // N_ROW
    cols_tile = FF // N_COL
    side_rows = rows_tile // BLK
    side_cols = cols_tile // BLK
    all_rows = stash_now.shape[0]

    def one_column(input_part, tile_set):
        in_v, in_i, out_v, out_i = tile_set
        in_v = unpair(in_v)
        out_v = unpair(out_v)
        hidden = jnp.zeros((all_rows, cols_tile), jnp.float32)
        gate_grad = jnp.zeros((all_rows, cols_tile), jnp.float32)
        for row_block in range(N_ROW):
            stash_cols = stash_now[:, row_block * rows_tile:(row_block + 1) * rows_tile]
            grad_cols = upstream[:, row_block * rows_tile:(row_block + 1) * rows_tile]
            hidden_part = tile_product(stash_cols, in_v[row_block], in_i[row_block, 0], in_i[row_block, 1], side_cols, forward_form)
            gate_part = tile_product(grad_cols, out_v[row_block], out_i[row_block, 0], out_i[row_block, 1], side_cols, forward_form)
            hidden = hidden + lax.optimization_barrier(hidden_part.astype(jnp.bfloat16)).astype(jnp.float32)
            gate_grad = gate_grad + lax.optimization_barrier(gate_part.astype(jnp.bfloat16)).astype(jnp.float32)
        hidden_grad = (gate_grad * gelu_slope(hidden)).astype(jnp.bfloat16)
        pieces_out = [tile_product(hidden_grad, in_v[row_block], in_i[row_block, 1], in_i[row_block, 0], side_rows, backward_form) for row_block in range(N_ROW)]
        column_term = jnp.concatenate(pieces_out, axis=1)
        return (input_part + lax.optimization_barrier(column_term.astype(jnp.bfloat16)).astype(jnp.float32), None)
    tile_set = (jnp.moveaxis(in_values, 1, 0), jnp.moveaxis(in_index, 1, 0), jnp.moveaxis(out_values, 1, 0), jnp.moveaxis(out_index, 1, 0))
    input_part, _ = lax.scan(one_column, jnp.zeros((all_rows, D), jnp.float32), tile_set)
    return (upstream.astype(jnp.float32) + input_part).astype(jnp.bfloat16)

def reference(x_stash, out_grad, in_values, in_index, out_values, out_index):
    all_rows = MICRO * MB_TOK
    upstream = out_grad.reshape(all_rows, D)
    last_section = layer_grad(x_stash[1].reshape(all_rows, D), upstream, in_values[1], in_index[1], out_values[1], out_index[1])
    first_section = layer_grad(x_stash[0].reshape(all_rows, D), last_section, in_values[0], in_index[0], out_values[0], out_index[0])
    return jnp.stack([first_section, last_section]).reshape(2, MICRO, MB_TOK, D)
```

```python
import functools

import jax
import jax.numpy as jnp
from jax import lax
from jax.experimental import pallas as pl
from jax.experimental.pallas import tpu as pltpu
from jax.sharding import PartitionSpec as P

LANES = 128
BLK = 64
PER_COL = 2
SWAP = [(0, 1), (1, 0)]
UNROLL = 16
SMEM = pl.BlockSpec(memory_space=pltpu.SMEM)
VMEM = pl.BlockSpec(memory_space=pltpu.VMEM)


def left_half(rows):
    return lax.broadcasted_iota(jnp.int32, (rows, LANES), 1) < BLK


def forward_kernel(count, *refs):
    index, x_ref, values = refs[:count], refs[count], refs[count + 1 : 2 * count + 1]
    out_ref, rows, blocks, even, odd = refs[2 * count + 1 :]
    tokens = blocks.shape[1]
    subs = blocks.shape[0] // 2
    left = left_half(tokens)
    for i in range(count):
        rows[...] = x_ref[:, i].reshape(rows.shape).astype(jnp.float32)
        for w in range(subs):
            both = rows[pl.ds(w, tokens, stride=subs), :]
            blocks[2 * w] = both.astype(jnp.bfloat16)
            blocks[2 * w + 1] = pltpu.roll(both, BLK, 1).astype(jnp.bfloat16)
        even[...] = jnp.zeros_like(even)
        odd[...] = jnp.zeros_like(odd)

        def multiply(pair, carry):
            first, second = 2 * pair, 2 * pair + 1
            picked = [blocks[index[i][0, n]][:, :BLK] for n in (first, second)]
            product = jnp.dot(
                jnp.concatenate(picked), values[i][pair], preferred_element_type=jnp.float32
            )
            even[index[i][1, first]] += product[:tokens]
            odd[index[i][1, second]] += product[tokens:]
            return carry

        lax.fori_loop(0, values[i].shape[0], multiply, 0, unroll=UNROLL)
        chunk = out_ref.shape[3] // LANES
        for j in range(even.shape[0] // 2):
            a, b = 2 * j, 2 * j + 1
            straight = jnp.where(left, even[a], odd[b])
            crossed = jnp.where(left, even[b], odd[a])
            total = straight + pltpu.roll(crossed, BLK, 1)
            lanes = slice((j % chunk) * LANES, (j % chunk + 1) * LANES)
            out_ref[j // chunk, i, :, lanes] = total.astype(jnp.bfloat16)


def forward(x, weights, n_row, ff_tile):
    count = len(weights)
    n_col, _, per, _ = x.shape
    tokens = n_col * PER_COL
    subs = per // PER_COL
    blocks_out = ff_tile // BLK
    return pl.pallas_call(
        functools.partial(forward_kernel, count),
        out_shape=jax.ShapeDtypeStruct((n_row, count, tokens, ff_tile // n_row), jnp.bfloat16),
        in_specs=[SMEM] * count + [VMEM] * (1 + count),
        out_specs=VMEM,
        scratch_shapes=[
            pltpu.VMEM((n_col * per, LANES), jnp.float32),
            pltpu.VMEM((2 * subs, tokens, LANES), jnp.bfloat16),
            pltpu.VMEM((blocks_out, tokens, LANES), jnp.float32),
            pltpu.VMEM((blocks_out, tokens, LANES), jnp.float32),
        ],
        compiler_params=pltpu.CompilerParams(vmem_limit_bytes=16 * 2**20),
        cost_estimate=pl.CostEstimate(
            flops=count * 10**9, bytes_accessed=count * 2 * 2**20, transcendentals=0
        ),
    )(*[w[0] for w in weights], x, *[w[1] for w in weights])


def backward_kernel(index, hidden_ref, values, out_ref, rows, lower, upper, total):
    tokens = lower.shape[1]
    subs = total.shape[0] // 2
    chunk = hidden_ref.shape[2] // LANES
    left = left_half(tokens)
    for j in range(lower.shape[0] // 2):
        lanes = slice((j % chunk) * LANES, (j % chunk + 1) * LANES)
        both = hidden_ref[j // chunk, :, lanes].astype(jnp.float32)
        turned = pltpu.roll(both, BLK, 1)
        lower[2 * j] = jnp.where(left, both, 0.0).astype(jnp.bfloat16)
        upper[2 * j + 1] = jnp.where(left, 0.0, both).astype(jnp.bfloat16)
        lower[2 * j + 1] = jnp.where(left, turned, 0.0).astype(jnp.bfloat16)
        upper[2 * j] = jnp.where(left, 0.0, turned).astype(jnp.bfloat16)
    total[...] = jnp.zeros_like(total)

    def multiply(pair, carry):
        first, second = 2 * pair, 2 * pair + 1
        picked = jnp.concatenate([lower[index[1, first]], upper[index[1, second]]])
        product = lax.dot_general(
            picked, values[pair], (((1,), (1,)), ((), ())), preferred_element_type=jnp.float32
        )
        total[index[0, first]] += product[:tokens]
        total[index[0, second]] += product[tokens:]
        return carry

    lax.fori_loop(0, values.shape[0], multiply, 0, unroll=UNROLL)
    for w in range(subs):
        both = jnp.concatenate([total[2 * w], total[2 * w + 1]], axis=1)
        rows[pl.ds(w, tokens, stride=subs), :] = both
    out_ref[...] = rows[...].astype(jnp.bfloat16).reshape(out_ref.shape)


def backward(hidden_grad, weights, n_col, width):
    tokens = hidden_grad.shape[1]
    ff_tile = hidden_grad.shape[0] * hidden_grad.shape[2]
    per = PER_COL * width // LANES
    return pl.pallas_call(
        backward_kernel,
        out_shape=jax.ShapeDtypeStruct((n_col, per, LANES), jnp.bfloat16),
        in_specs=[SMEM, VMEM, VMEM],
        out_specs=VMEM,
        scratch_shapes=[
            pltpu.VMEM((n_col * per, LANES), jnp.float32),
            pltpu.VMEM((ff_tile // BLK, tokens, LANES), jnp.bfloat16),
            pltpu.VMEM((ff_tile // BLK, tokens, LANES), jnp.bfloat16),
            pltpu.VMEM((width // BLK, tokens, BLK), jnp.float32),
        ],
        compiler_params=pltpu.CompilerParams(vmem_limit_bytes=16 * 2**20),
        cost_estimate=pl.CostEstimate(flops=10**9, bytes_accessed=2 * 2**20, transcendentals=0),
    )(weights[0], hidden_grad, weights[1])


def gelu_slope(hidden):
    return (
        0.5 * (1.0 + lax.erf(hidden * 0.7071067811865476))
        + hidden * jnp.exp(-0.5 * hidden * hidden) * 0.3989422804014327
    )


def local(n_row, n_col, ff, x_stash, out_grad, in_values, in_index, out_values, out_index):
    section = lax.axis_index("section")
    is_last = section == 1
    width = x_stash.shape[3]
    ff_tile = ff // n_col
    per = PER_COL * width // LANES

    def exchange(v, axis):
        return lax.all_to_all(v, axis, 0, 0)

    def gather(v, axis):
        return exchange(jnp.broadcast_to(v[None], (lax.axis_size(axis),) + v.shape), axis)

    def products(x, weights):
        return forward(x, weights, n_row, ff_tile)

    def row_sums(parts):
        return jnp.sum(exchange(parts, "row").astype(jnp.float32), axis=0)

    def finish(hidden, gate_grad, g, w_in):
        hidden_grad = (gate_grad * gelu_slope(hidden)).astype(jnp.bfloat16)
        part = exchange(backward(gather(hidden_grad, "row"), w_in, n_col, width), "col")
        return (g.astype(jnp.float32) + jnp.sum(part.astype(jnp.float32), axis=0)).astype(jnp.bfloat16)

    def swap(v):
        return lax.ppermute(v, "section", SWAP)

    def shard_of(v, start):
        return lax.dynamic_slice_in_dim(v, start, PER_COL, 0).reshape(per, LANES)

    in_own, out_own = in_values[0, 0, 0], out_values[0, 0, 0]
    in_at, out_at = in_index[0, 0, 0], out_index[0, 0, 0]
    places = jnp.concatenate([in_at, out_at]).astype(jnp.bfloat16)
    places = jnp.pad(places, ((0, 12), (0, 0)))
    mine = shard_of(x_stash[0, 0], PER_COL * section)
    came = swap(jnp.concatenate([shard_of(x_stash[0, 0], PER_COL - PER_COL * section), places]))
    other = came[:per]
    at_oth = came[per : per + 4].astype(jnp.int32)
    g1 = shard_of(out_grad[0], PER_COL * section)
    shards = jnp.stack([jnp.where(is_last, mine, other), g1, jnp.where(is_last, other, mine)])
    shards, in_sent, out_sent = lax.optimization_barrier((shards, in_own, out_own))
    first = gather(shards, "col")
    in_oth, out_oth = swap(in_sent), swap(out_sent)
    own = ((in_at, in_own), (out_at, out_own))
    oth = ((at_oth[:2], in_oth), (at_oth[2:], out_oth))

    def later_core(own, oth, first, g1):
        w1, w0 = own, oth
        sums = row_sums(products(first[:, :2], w1))
        g0 = finish(sums[0], sums[1], g1, w1[0])
        hidden0 = products(first[:, 2:], w0[:1])
        gate0 = products(gather(g0[None], "col"), w0[1:])
        sums = row_sums(jnp.concatenate([hidden0, gate0], axis=1))
        return g0, finish(sums[0], sums[1], g0, w0[0])

    def earlier_core(own, oth, first, g1):
        w1, w0 = oth, own
        sums = row_sums(products(first, w1 + w0[:1]))
        g0 = finish(sums[0], sums[1], g1, w1[0])
        gate0 = row_sums(products(gather(g0[None], "col"), w0[1:]))[0]
        return g0, finish(sums[2], gate0, g0, w0[0])

    g0, last = lax.cond(is_last, later_core, earlier_core, own, oth, first, g1)

    kept = jnp.where(is_last, g0, last)
    came = swap(jnp.where(is_last, last, g0))
    result = jnp.where(is_last, jnp.stack([came, kept]), jnp.stack([kept, came]))
    return result.reshape(1, 1, 2 * PER_COL, width)


def solution(mesh):
    in_specs = (
        P("section", None, "col", "row"),
        P(None, "col", "row"),
        P("section", "row", "col", None, None, None),
        P("section", "row", "col", None, None),
        P("section", "row", "col", None, None, None),
        P("section", "row", "col", None, None),
    )
    out_specs = P("section", None, "col", "row")
    body = functools.partial(local, mesh.shape["row"], mesh.shape["col"], 65536)
    return jax.shard_map(body, mesh=mesh, in_specs=in_specs, out_specs=out_specs, check_vma=False)
```

```python
import functools

import jax
import jax.numpy as jnp
from jax import lax
from jax.experimental import pallas as pl
from jax.experimental.pallas import tpu as pltpu
from jax.sharding import PartitionSpec as P

LANES = 128
BLK = 64
PER_COL = 2
SWAP = [(0, 1), (1, 0)]
UNROLL = 16
SMEM = pl.BlockSpec(memory_space=pltpu.SMEM)
VMEM = pl.BlockSpec(memory_space=pltpu.VMEM)


def left_half(rows):
    return lax.broadcasted_iota(jnp.int32, (rows, LANES), 1) < BLK


def forward_kernel(count, *refs):
    index, x_ref, values = refs[:count], refs[count], refs[count + 1 : 2 * count + 1]
    out_ref, rows, blocks, even, odd = refs[2 * count + 1 :]
    tokens = blocks.shape[1]
    subs = blocks.shape[0] // 2
    left = left_half(tokens)
    for i in range(count):
        rows[...] = x_ref[:, i].reshape(rows.shape).astype(jnp.float32)
        for w in range(subs):
            both = rows[pl.ds(w, tokens, stride=subs), :]
            blocks[2 * w] = both.astype(jnp.bfloat16)
            blocks[2 * w + 1] = pltpu.roll(both, BLK, 1).astype(jnp.bfloat16)
        even[...] = jnp.zeros_like(even)
        odd[...] = jnp.zeros_like(odd)

        def multiply(pair, carry):
            first, second = 2 * pair, 2 * pair + 1
            picked = [blocks[index[i][0, n]][:, :BLK] for n in (first, second)]
            product = jnp.dot(
                jnp.concatenate(picked), values[i][pair], preferred_element_type=jnp.float32
            )
            even[index[i][1, first]] += product[:tokens]
            odd[index[i][1, second]] += product[tokens:]
            return carry

        lax.fori_loop(0, values[i].shape[0], multiply, 0, unroll=UNROLL)
        chunk = out_ref.shape[3] // LANES
        for j in range(even.shape[0] // 2):
            a, b = 2 * j, 2 * j + 1
            straight = jnp.where(left, even[a], odd[b])
            crossed = jnp.where(left, even[b], odd[a])
            total = straight + pltpu.roll(crossed, BLK, 1)
            lanes = slice((j % chunk) * LANES, (j % chunk + 1) * LANES)
            out_ref[j // chunk, i, :, lanes] = total.astype(jnp.bfloat16)


def forward(x, weights, n_row, ff_tile):
    count = len(weights)
    n_col, _, per, _ = x.shape
    tokens = n_col * PER_COL
    subs = per // PER_COL
    blocks_out = ff_tile // BLK
    return pl.pallas_call(
        functools.partial(forward_kernel, count),
        out_shape=jax.ShapeDtypeStruct((n_row, count, tokens, ff_tile // n_row), jnp.bfloat16),
        in_specs=[SMEM] * count + [VMEM] * (1 + count),
        out_specs=VMEM,
        scratch_shapes=[
            pltpu.VMEM((n_col * per, LANES), jnp.float32),
            pltpu.VMEM((2 * subs, tokens, LANES), jnp.bfloat16),
            pltpu.VMEM((blocks_out, tokens, LANES), jnp.float32),
            pltpu.VMEM((blocks_out, tokens, LANES), jnp.float32),
        ],
        compiler_params=pltpu.CompilerParams(vmem_limit_bytes=16 * 2**20),
        cost_estimate=pl.CostEstimate(
            flops=count * 10**9, bytes_accessed=count * 2 * 2**20, transcendentals=0
        ),
    )(*[w[0] for w in weights], x, *[w[1] for w in weights])


def backward_kernel(index, hidden_ref, values, out_ref, rows, lower, upper, total):
    tokens = lower.shape[1]
    subs = total.shape[0] // 2
    chunk = hidden_ref.shape[2] // LANES
    left = left_half(tokens)
    for j in range(lower.shape[0] // 2):
        lanes = slice((j % chunk) * LANES, (j % chunk + 1) * LANES)
        both = hidden_ref[j // chunk, :, lanes].astype(jnp.float32)
        turned = pltpu.roll(both, BLK, 1)
        lower[2 * j] = jnp.where(left, both, 0.0).astype(jnp.bfloat16)
        upper[2 * j + 1] = jnp.where(left, 0.0, both).astype(jnp.bfloat16)
        lower[2 * j + 1] = jnp.where(left, turned, 0.0).astype(jnp.bfloat16)
        upper[2 * j] = jnp.where(left, 0.0, turned).astype(jnp.bfloat16)
    total[...] = jnp.zeros_like(total)

    def multiply(pair, carry):
        first, second = 2 * pair, 2 * pair + 1
        picked = jnp.concatenate([lower[index[1, first]], upper[index[1, second]]])
        product = lax.dot_general(
            picked, values[pair], (((1,), (1,)), ((), ())), preferred_element_type=jnp.float32
        )
        total[index[0, first]] += product[:tokens]
        total[index[0, second]] += product[tokens:]
        return carry

    lax.fori_loop(0, values.shape[0], multiply, 0, unroll=UNROLL)
    for w in range(subs):
        both = jnp.concatenate([total[2 * w], total[2 * w + 1]], axis=1)
        rows[pl.ds(w, tokens, stride=subs), :] = both
    out_ref[...] = rows[...].astype(jnp.bfloat16).reshape(out_ref.shape)


def backward(hidden_grad, weights, n_col, width):
    tokens = hidden_grad.shape[1]
    ff_tile = hidden_grad.shape[0] * hidden_grad.shape[2]
    per = PER_COL * width // LANES
    return pl.pallas_call(
        backward_kernel,
        out_shape=jax.ShapeDtypeStruct((n_col, per, LANES), jnp.bfloat16),
        in_specs=[SMEM, VMEM, VMEM],
        out_specs=VMEM,
        scratch_shapes=[
            pltpu.VMEM((n_col * per, LANES), jnp.float32),
            pltpu.VMEM((ff_tile // BLK, tokens, LANES), jnp.bfloat16),
            pltpu.VMEM((ff_tile // BLK, tokens, LANES), jnp.bfloat16),
            pltpu.VMEM((width // BLK, tokens, BLK), jnp.float32),
        ],
        compiler_params=pltpu.CompilerParams(vmem_limit_bytes=16 * 2**20),
        cost_estimate=pl.CostEstimate(flops=10**9, bytes_accessed=2 * 2**20, transcendentals=0),
    )(weights[0], hidden_grad, weights[1])


def gelu_slope(hidden):
    return (
        0.5 * (1.0 + lax.erf(hidden * 0.7071067811865476))
        + hidden * jnp.exp(-0.5 * hidden * hidden) * 0.3989422804014327
    )


def local(n_row, n_col, ff, x_stash, out_grad, in_values, in_index, out_values, out_index):
    section = lax.axis_index("section")
    is_last = section == 1
    width = x_stash.shape[3]
    ff_tile = ff // n_col
    per = PER_COL * width // LANES

    def exchange(v, axis):
        return lax.all_to_all(v, axis, 0, 0)

    def gather(v, axis):
        return exchange(jnp.broadcast_to(v[None], (lax.axis_size(axis),) + v.shape), axis)

    def products(x, weights):
        return forward(x, weights, n_row, ff_tile)

    def row_sums(parts):
        return jnp.sum(exchange(parts, "row").astype(jnp.float32), axis=0)

    def add(g, part):
        return (g.astype(jnp.float32) + part).astype(jnp.bfloat16)

    def col_sum(sums, w_in):
        hidden_grad = (sums[1] * gelu_slope(sums[0])).astype(jnp.bfloat16)
        part = exchange(backward(gather(hidden_grad, "row"), w_in, n_col, width), "col")
        return jnp.sum(part.astype(jnp.float32), axis=0)

    def swap(v):
        return lax.ppermute(v, "section", SWAP)

    def shard_of(v, start):
        return lax.dynamic_slice_in_dim(v, start, PER_COL, 0).reshape(per, LANES)

    in_own, out_own = in_values[0, 0, 0], out_values[0, 0, 0]
    in_at, out_at = in_index[0, 0, 0], out_index[0, 0, 0]
    mine = shard_of(x_stash[0, 0], PER_COL * section)
    other = swap(shard_of(x_stash[0, 0], PER_COL - PER_COL * section))
    g1 = shard_of(out_grad[0], PER_COL * section)
    shards = jnp.stack([jnp.where(is_last, mine, other), g1])
    x0 = jnp.where(is_last, other, mine)
    shards, in_sent, out_sent, in_at, out_at = lax.optimization_barrier(
        (shards, in_own, out_own, in_at, out_at)
    )
    first = gather(shards, "col")
    in_oth, out_oth = swap(in_sent), swap(out_sent)
    at_oth = swap(jnp.concatenate([in_at, out_at]))
    own = ((in_at, in_own), (out_at, out_own))
    oth = ((at_oth[:2], in_oth), (at_oth[2:], out_oth))

    def layers(w1, w0, first, g1, x0):
        g0 = add(g1, col_sum(row_sums(products(first, w1)), w1[0]))
        second = gather(jnp.stack([x0, g0]), "col")
        return g0, col_sum(row_sums(products(second, w0)), w0[0])

    def later_core(own, oth, *rest):
        return layers(own, oth, *rest)

    def earlier_core(own, oth, *rest):
        return layers(oth, own, *rest)

    g0, part = lax.cond(is_last, later_core, earlier_core, own, oth, first, g1, x0)
    last = add(g0, part)

    kept = jnp.where(is_last, g0, last)
    came = swap(jnp.where(is_last, last, g0))
    result = jnp.where(is_last, jnp.stack([came, kept]), jnp.stack([kept, came]))
    return result.reshape(1, 1, 2 * PER_COL, width)


def solution(mesh):
    in_specs = (
        P("section", None, "col", "row"),
        P(None, "col", "row"),
        P("section", "row", "col", None, None, None),
        P("section", "row", "col", None, None),
        P("section", "row", "col", None, None, None),
        P("section", "row", "col", None, None),
    )
    out_specs = P("section", None, "col", "row")
    body = functools.partial(local, mesh.shape["row"], mesh.shape["col"], 65536)
    return jax.shard_map(body, mesh=mesh, in_specs=in_specs, out_specs=out_specs, check_vma=False)
```

```python
import functools

import jax
import jax.numpy as jnp
from jax import lax
from jax.experimental import pallas as pl
from jax.experimental.pallas import tpu as pltpu
from jax.sharding import PartitionSpec as P

LANES = 128
BLK = 64
PER_COL = 2
SWAP = [(0, 1), (1, 0)]
UNROLL = 16
SMEM = pl.BlockSpec(memory_space=pltpu.SMEM)
VMEM = pl.BlockSpec(memory_space=pltpu.VMEM)


def left_half(rows):
    return lax.broadcasted_iota(jnp.int32, (rows, LANES), 1) < BLK


def forward_kernel(count, ahead, *refs):
    index, x_ref, values = refs[:count], refs[count], refs[count + 1 : 2 * count + 1]
    out_ref, rows, blocks, total = refs[2 * count + 1 + ahead :]
    tokens = blocks.shape[1]
    subs = blocks.shape[0] // 2
    left = left_half(tokens)
    if ahead:
        out_ref[:, 0] = refs[2 * count + 1][:, 0]
    for i in range(count):
        rows[...] = x_ref[:, i].reshape(rows.shape).astype(jnp.float32)
        for w in range(subs):
            both = rows[pl.ds(w, tokens, stride=subs), :]
            blocks[2 * w] = both.astype(jnp.bfloat16)
            blocks[2 * w + 1] = pltpu.roll(both, BLK, 1).astype(jnp.bfloat16)
        total[...] = jnp.zeros_like(total)

        def multiply(pair, carry):
            first, second = 2 * pair, 2 * pair + 1
            picked = [blocks[index[i][0, n]][:, :BLK] for n in (first, second)]
            product = jnp.dot(
                jnp.concatenate(picked), values[i][pair], preferred_element_type=jnp.float32
            )
            total[index[i][1, first]] += jnp.where(left, product[:tokens], 0.0)
            total[index[i][1, second]] += jnp.where(left, 0.0, product[tokens:])
            return carry

        lax.fori_loop(0, values[i].shape[0], multiply, 0, unroll=UNROLL)
        chunk = out_ref.shape[3] // LANES
        for j in range(total.shape[0] // 2):
            a, b = total[2 * j], total[2 * j + 1]
            summed = jnp.where(left, a, b) + pltpu.roll(jnp.where(left, b, a), BLK, 1)
            lanes = slice((j % chunk) * LANES, (j % chunk + 1) * LANES)
            out_ref[j // chunk, i + ahead, :, lanes] = summed.astype(jnp.bfloat16)


def forward(x, weights, n_row, ff_tile, prior=None):
    count = len(weights)
    ahead = 0 if prior is None else 1
    n_col, _, per, _ = x.shape
    tokens = n_col * PER_COL
    subs = per // PER_COL
    return pl.pallas_call(
        functools.partial(forward_kernel, count, ahead),
        out_shape=jax.ShapeDtypeStruct(
            (n_row, count + ahead, tokens, ff_tile // n_row), jnp.bfloat16
        ),
        in_specs=[SMEM] * count + [VMEM] * (1 + count + ahead),
        out_specs=VMEM,
        scratch_shapes=[
            pltpu.VMEM((n_col * per, LANES), jnp.float32),
            pltpu.VMEM((2 * subs, tokens, LANES), jnp.bfloat16),
            pltpu.VMEM((ff_tile // BLK, tokens, LANES), jnp.float32),
        ],
        compiler_params=pltpu.CompilerParams(vmem_limit_bytes=16 * 2**20),
        cost_estimate=pl.CostEstimate(
            flops=count * 10**9, bytes_accessed=count * 2 * 2**20, transcendentals=0
        ),
    )(*[w[0] for w in weights], x, *[w[1] for w in weights], *([prior] if ahead else []))


def backward_kernel(ahead, index, hidden_ref, values, *refs):
    out_ref, rows, lower, upper, total = refs[ahead:]
    tokens = lower.shape[1]
    subs = total.shape[0] // 2
    chunk = hidden_ref.shape[2] // LANES
    left = left_half(tokens)
    for j in range(lower.shape[0] // 2):
        lanes = slice((j % chunk) * LANES, (j % chunk + 1) * LANES)
        both = hidden_ref[j // chunk, :, lanes].astype(jnp.float32)
        turned = pltpu.roll(both, BLK, 1)
        lower[2 * j] = jnp.where(left, both, 0.0).astype(jnp.bfloat16)
        upper[2 * j + 1] = jnp.where(left, 0.0, both).astype(jnp.bfloat16)
        lower[2 * j + 1] = jnp.where(left, turned, 0.0).astype(jnp.bfloat16)
        upper[2 * j] = jnp.where(left, 0.0, turned).astype(jnp.bfloat16)
    total[...] = jnp.zeros_like(total)

    def multiply(pair, carry):
        first, second = 2 * pair, 2 * pair + 1
        picked = jnp.concatenate([lower[index[1, first]], upper[index[1, second]]])
        product = lax.dot_general(
            picked, values[pair], (((1,), (1,)), ((), ())), preferred_element_type=jnp.float32
        )
        total[index[0, first]] += product[:tokens]
        total[index[0, second]] += product[tokens:]
        return carry

    lax.fori_loop(0, values.shape[0], multiply, 0, unroll=UNROLL)
    for w in range(subs):
        both = jnp.concatenate([total[2 * w], total[2 * w + 1]], axis=1)
        rows[pl.ds(w, tokens, stride=subs), :] = both
    n_col, _, per, _ = out_ref.shape
    out_ref[:, 0] = rows[...].astype(jnp.bfloat16).reshape(n_col, per, LANES)
    if ahead:
        out_ref[:, 1] = jnp.broadcast_to(refs[0][...][None], (n_col, per, LANES))


def backward(hidden_grad, weights, n_col, width, shard=None):
    tokens = hidden_grad.shape[1]
    ff_tile = hidden_grad.shape[0] * hidden_grad.shape[2]
    per = PER_COL * width // LANES
    ahead = 0 if shard is None else 1
    return pl.pallas_call(
        functools.partial(backward_kernel, ahead),
        out_shape=jax.ShapeDtypeStruct((n_col, 1 + ahead, per, LANES), jnp.bfloat16),
        in_specs=[SMEM] + [VMEM] * (2 + ahead),
        out_specs=VMEM,
        scratch_shapes=[
            pltpu.VMEM((n_col * per, LANES), jnp.float32),
            pltpu.VMEM((ff_tile // BLK, tokens, LANES), jnp.bfloat16),
            pltpu.VMEM((ff_tile // BLK, tokens, LANES), jnp.bfloat16),
            pltpu.VMEM((width // BLK, tokens, BLK), jnp.float32),
        ],
        compiler_params=pltpu.CompilerParams(vmem_limit_bytes=16 * 2**20),
        cost_estimate=pl.CostEstimate(flops=10**9, bytes_accessed=2 * 2**20, transcendentals=0),
    )(weights[0], hidden_grad, weights[1], *([shard] if ahead else []))


def gelu_slope(hidden):
    return (
        0.5 * (1.0 + lax.erf(hidden * 0.7071067811865476))
        + hidden * jnp.exp(-0.5 * hidden * hidden) * 0.3989422804014327
    )


def local(n_row, n_col, ff, x_stash, out_grad, in_values, in_index, out_values, out_index):
    section = lax.axis_index("section")
    is_last = section == 1
    width = x_stash.shape[3]
    ff_tile = ff // n_col
    per = PER_COL * width // LANES

    def exchange(v, axis):
        return lax.all_to_all(v, axis, 0, 0)

    def gather(v, axis):
        return exchange(jnp.broadcast_to(v[None], (lax.axis_size(axis),) + v.shape), axis)

    def products(x, weights, prior=None):
        return forward(x, weights, n_row, ff_tile, prior)

    def row_sums(parts):
        return jnp.sum(exchange(parts, "row").astype(jnp.float32), axis=0)

    def add(g, part):
        return (g.astype(jnp.float32) + part).astype(jnp.bfloat16)

    def scatter(sums, w_in, shard=None):
        hidden_grad = (sums[1] * gelu_slope(sums[0])).astype(jnp.bfloat16)
        return exchange(backward(gather(hidden_grad, "row"), w_in, n_col, width, shard), "col")

    def total(parts):
        return jnp.sum(parts[:, 0].astype(jnp.float32), axis=0)

    def swap(v):
        return lax.ppermute(v, "section", SWAP)

    def shard_of(v, start):
        return lax.dynamic_slice_in_dim(v, start, PER_COL, 0).reshape(per, LANES)

    in_own, out_own = in_values[0, 0, 0], out_values[0, 0, 0]
    in_at, out_at = in_index[0, 0, 0], out_index[0, 0, 0]
    mine = shard_of(x_stash[0, 0], PER_COL * section)
    other = swap(shard_of(x_stash[0, 0], PER_COL - PER_COL * section))
    g1 = shard_of(out_grad[0], PER_COL * section)
    shards = jnp.stack([jnp.where(is_last, mine, other), g1])
    x0 = jnp.where(is_last, other, mine)
    shards, in_at, out_at = lax.optimization_barrier((shards, in_at, out_at))
    first = gather(shards, "col")
    at_oth = swap(jnp.concatenate([in_at, out_at]))
    at_oth, in_sent, out_sent = lax.optimization_barrier((at_oth, in_own, out_own))
    in_oth, out_oth = swap(in_sent), swap(out_sent)
    own = ((in_at, in_own), (out_at, out_own))
    oth = ((at_oth[:2], in_oth), (at_oth[2:], out_oth))

    def layers(w1, w0, first, g1, x0):
        parts = scatter(row_sums(products(first, w1)), w1[0], x0)
        g0 = add(g1, total(parts))
        second = gather(g0[None], "col")
        hidden0 = products(parts[:, 1:], w0[:1])
        return g0, total(scatter(row_sums(products(second, w0[1:], hidden0)), w0[0]))

    def later_core(own, oth, *rest):
        return layers(own, oth, *rest)

    def earlier_core(own, oth, *rest):
        return layers(oth, own, *rest)

    g0, part = lax.cond(is_last, later_core, earlier_core, own, oth, first, g1, x0)
    last = add(g0, part)

    kept = jnp.where(is_last, g0, last)
    came = swap(jnp.where(is_last, last, g0))
    result = jnp.where(is_last, jnp.stack([came, kept]), jnp.stack([kept, came]))
    return result.reshape(1, 1, 2 * PER_COL, width)


def solution(mesh):
    in_specs = (
        P("section", None, "col", "row"),
        P(None, "col", "row"),
        P("section", "row", "col", None, None, None),
        P("section", "row", "col", None, None),
        P("section", "row", "col", None, None, None),
        P("section", "row", "col", None, None),
    )
    out_specs = P("section", None, "col", "row")
    body = functools.partial(local, mesh.shape["row"], mesh.shape["col"], 65536)
    return jax.shard_map(body, mesh=mesh, in_specs=in_specs, out_specs=out_specs, check_vma=False)
```

```python
import functools

import jax
import jax.numpy as jnp
from jax import lax
from jax.experimental import pallas as pl
from jax.experimental.pallas import tpu as pltpu
from jax.sharding import PartitionSpec as P

LANES = 128
BLK = 64
PER_COL = 2
SWAP = [(0, 1), (1, 0)]
UNROLL = 16
SMEM = pl.BlockSpec(memory_space=pltpu.SMEM)
VMEM = pl.BlockSpec(memory_space=pltpu.VMEM)


def left_half(rows):
    return lax.broadcasted_iota(jnp.int32, (rows, LANES), 1) < BLK


def forward_kernel(count, ahead, *refs):
    index, x_ref, values = refs[:count], refs[count], refs[count + 1 : 2 * count + 1]
    out_ref, rows, blocks, even, odd = refs[2 * count + 1 + ahead :]
    tokens = blocks.shape[1]
    subs = blocks.shape[0] // 2
    left = left_half(tokens)
    if ahead:
        out_ref[:, 0] = refs[2 * count + 1][:, 0]
    for i in range(count):
        rows[...] = x_ref[:, i].reshape(rows.shape).astype(jnp.float32)
        for w in range(subs):
            both = rows[pl.ds(w, tokens, stride=subs), :]
            blocks[2 * w] = both.astype(jnp.bfloat16)
            blocks[2 * w + 1] = pltpu.roll(both, BLK, 1).astype(jnp.bfloat16)
        even[...] = jnp.zeros_like(even)
        odd[...] = jnp.zeros_like(odd)

        def multiply(pair, carry):
            first, second = 2 * pair, 2 * pair + 1
            picked = [blocks[index[i][0, n]][:, :BLK] for n in (first, second)]
            product = jnp.dot(
                jnp.concatenate(picked), values[i][pair], preferred_element_type=jnp.float32
            )
            even[index[i][1, first]] += product[:tokens]
            odd[index[i][1, second]] += product[tokens:]
            return carry

        lax.fori_loop(0, values[i].shape[0], multiply, 0, unroll=UNROLL)
        chunk = out_ref.shape[3] // LANES
        for j in range(even.shape[0] // 2):
            a, b = 2 * j, 2 * j + 1
            straight = jnp.where(left, even[a], odd[b])
            crossed = jnp.where(left, even[b], odd[a])
            summed = straight + pltpu.roll(crossed, BLK, 1)
            lanes = slice((j % chunk) * LANES, (j % chunk + 1) * LANES)
            out_ref[j // chunk, i + ahead, :, lanes] = summed.astype(jnp.bfloat16)


def forward(x, weights, n_row, ff_tile, prior=None):
    count = len(weights)
    ahead = 0 if prior is None else 1
    n_col, _, per, _ = x.shape
    tokens = n_col * PER_COL
    subs = per // PER_COL
    return pl.pallas_call(
        functools.partial(forward_kernel, count, ahead),
        out_shape=jax.ShapeDtypeStruct(
            (n_row, count + ahead, tokens, ff_tile // n_row), jnp.bfloat16
        ),
        in_specs=[SMEM] * count + [VMEM] * (1 + count + ahead),
        out_specs=VMEM,
        scratch_shapes=[
            pltpu.VMEM((n_col * per, LANES), jnp.float32),
            pltpu.VMEM((2 * subs, tokens, LANES), jnp.bfloat16),
            pltpu.VMEM((ff_tile // BLK, tokens, LANES), jnp.float32),
            pltpu.VMEM((ff_tile // BLK, tokens, LANES), jnp.float32),
        ],
        compiler_params=pltpu.CompilerParams(vmem_limit_bytes=16 * 2**20),
        cost_estimate=pl.CostEstimate(
            flops=count * 10**9, bytes_accessed=count * 2 * 2**20, transcendentals=0
        ),
    )(*[w[0] for w in weights], x, *[w[1] for w in weights], *([prior] if ahead else []))


def backward_kernel(index, hidden_ref, values, out_ref, rows, lower, upper, total):
    tokens = lower.shape[1]
    subs = total.shape[0] // 2
    chunk = hidden_ref.shape[2] // LANES
    left = left_half(tokens)
    for j in range(lower.shape[0] // 2):
        lanes = slice((j % chunk) * LANES, (j % chunk + 1) * LANES)
        both = hidden_ref[j // chunk, :, lanes].astype(jnp.float32)
        turned = pltpu.roll(both, BLK, 1)
        lower[2 * j] = jnp.where(left, both, 0.0).astype(jnp.bfloat16)
        upper[2 * j + 1] = jnp.where(left, 0.0, both).astype(jnp.bfloat16)
        lower[2 * j + 1] = jnp.where(left, turned, 0.0).astype(jnp.bfloat16)
        upper[2 * j] = jnp.where(left, 0.0, turned).astype(jnp.bfloat16)
    total[...] = jnp.zeros_like(total)

    def multiply(pair, carry):
        first, second = 2 * pair, 2 * pair + 1
        picked = jnp.concatenate([lower[index[1, first]], upper[index[1, second]]])
        product = lax.dot_general(
            picked, values[pair], (((1,), (1,)), ((), ())), preferred_element_type=jnp.float32
        )
        total[index[0, first]] += product[:tokens]
        total[index[0, second]] += product[tokens:]
        return carry

    lax.fori_loop(0, values.shape[0], multiply, 0, unroll=UNROLL)
    for w in range(subs):
        both = jnp.concatenate([total[2 * w], total[2 * w + 1]], axis=1)
        rows[pl.ds(w, tokens, stride=subs), :] = both
    out_ref[...] = rows[...].astype(jnp.bfloat16).reshape(out_ref.shape)


def backward(hidden_grad, weights, n_col, width):
    tokens = hidden_grad.shape[1]
    ff_tile = hidden_grad.shape[0] * hidden_grad.shape[2]
    per = PER_COL * width // LANES
    return pl.pallas_call(
        backward_kernel,
        out_shape=jax.ShapeDtypeStruct((n_col, per, LANES), jnp.bfloat16),
        in_specs=[SMEM, VMEM, VMEM],
        out_specs=VMEM,
        scratch_shapes=[
            pltpu.VMEM((n_col * per, LANES), jnp.float32),
            pltpu.VMEM((ff_tile // BLK, tokens, LANES), jnp.bfloat16),
            pltpu.VMEM((ff_tile // BLK, tokens, LANES), jnp.bfloat16),
            pltpu.VMEM((width // BLK, tokens, BLK), jnp.float32),
        ],
        compiler_params=pltpu.CompilerParams(vmem_limit_bytes=16 * 2**20),
        cost_estimate=pl.CostEstimate(flops=10**9, bytes_accessed=2 * 2**20, transcendentals=0),
    )(weights[0], hidden_grad, weights[1])


def gelu_slope(hidden):
    return (
        0.5 * (1.0 + lax.erf(hidden * 0.7071067811865476))
        + hidden * jnp.exp(-0.5 * hidden * hidden) * 0.3989422804014327
    )


def local(n_row, n_col, ff, x_stash, out_grad, in_values, in_index, out_values, out_index):
    section = lax.axis_index("section")
    is_last = section == 1
    width = x_stash.shape[3]
    ff_tile = ff // n_col
    per = PER_COL * width // LANES

    def exchange(v, axis):
        return lax.all_to_all(v, axis, 0, 0)

    def gather(v, axis):
        return exchange(jnp.broadcast_to(v[None], (lax.axis_size(axis),) + v.shape), axis)

    def products(x, weights, prior=None):
        return forward(x, weights, n_row, ff_tile, prior)

    def row_sums(parts):
        return jnp.sum(exchange(parts, "row").astype(jnp.float32), axis=0)

    def add(g, part):
        return (g.astype(jnp.float32) + part).astype(jnp.bfloat16)

    def col_sum(sums, w_in):
        hidden_grad = (sums[1] * gelu_slope(sums[0])).astype(jnp.bfloat16)
        part = exchange(backward(gather(hidden_grad, "row"), w_in, n_col, width), "col")
        return jnp.sum(part.astype(jnp.float32), axis=0)

    def swap(v):
        return lax.ppermute(v, "section", SWAP)

    def shard_of(v, start):
        return lax.dynamic_slice_in_dim(v, start, PER_COL, 0).reshape(per, LANES)

    in_own, out_own = in_values[0, 0, 0], out_values[0, 0, 0]
    in_at, out_at = in_index[0, 0, 0], out_index[0, 0, 0]
    places = jnp.concatenate([in_at, out_at]).astype(jnp.bfloat16)
    places = jnp.pad(places, ((0, 12), (0, 0)))
    mine = shard_of(x_stash[0, 0], PER_COL * section)
    came = swap(jnp.concatenate([shard_of(x_stash[0, 0], PER_COL - PER_COL * section), places]))
    other = came[:per]
    at_oth = came[per : per + 4].astype(jnp.int32)
    g1 = shard_of(out_grad[0], PER_COL * section)
    shards = jnp.stack([jnp.where(is_last, mine, other), g1, jnp.where(is_last, other, mine)])
    shards, in_sent, out_sent = lax.optimization_barrier((shards, in_own, out_own))
    first = gather(shards, "col")
    in_oth, out_oth = swap(in_sent), swap(out_sent)
    own = ((in_at, in_own), (out_at, out_own))
    oth = ((at_oth[:2], in_oth), (at_oth[2:], out_oth))

    def layers(w1, w0, first, g1):
        g0 = add(g1, col_sum(row_sums(products(first[:, :2], w1)), w1[0]))
        second = gather(g0[None], "col")
        hidden0 = products(first[:, 2:], w0[:1])
        return g0, col_sum(row_sums(products(second, w0[1:], hidden0)), w0[0])

    def later_core(own, oth, *rest):
        return layers(own, oth, *rest)

    def earlier_core(own, oth, *rest):
        return layers(oth, own, *rest)

    g0, part = lax.cond(is_last, later_core, earlier_core, own, oth, first, g1)
    last = add(g0, part)

    kept = jnp.where(is_last, g0, last)
    came = swap(jnp.where(is_last, last, g0))
    result = jnp.where(is_last, jnp.stack([came, kept]), jnp.stack([kept, came]))
    return result.reshape(1, 1, 2 * PER_COL, width)


def solution(mesh):
    in_specs = (
        P("section", None, "col", "row"),
        P(None, "col", "row"),
        P("section", "row", "col", None, None, None),
        P("section", "row", "col", None, None),
        P("section", "row", "col", None, None, None),
        P("section", "row", "col", None, None),
    )
    out_specs = P("section", None, "col", "row")
    body = functools.partial(local, mesh.shape["row"], mesh.shape["col"], 65536)
    return jax.shard_map(body, mesh=mesh, in_specs=in_specs, out_specs=out_specs, check_vma=False)
```

```python
import functools

import jax
import jax.numpy as jnp
from jax import lax
from jax.experimental import pallas as pl
from jax.experimental.pallas import tpu as pltpu
from jax.sharding import PartitionSpec as P

LANES = 128
BLK = 64
PER_COL = 2
SWAP = [(0, 1), (1, 0)]
UNROLL = 32
VMEM = pl.BlockSpec(memory_space=pltpu.VMEM)
ANY = pl.BlockSpec(memory_space=pl.ANY)


def left_half(rows):
    return lax.broadcasted_iota(jnp.int32, (rows, LANES), 1) < BLK


def fetches(count, index_in, values_in, index, values, sems):
    copies = [
        pltpu.make_async_copy(source, target.at[i], sems.at[k, i])
        for i in range(count)
        for k, (source, target) in enumerate([(index_in[i], index), (values_in[i], values)])
    ]
    for copy in copies:
        copy.start()
    return copies


def fetch_scratch(count, weights):
    return [
        pltpu.SMEM((count,) + weights[0][0].shape, jnp.int32),
        pltpu.VMEM((count,) + weights[0][1].shape, jnp.bfloat16),
        pltpu.SemaphoreType.DMA((2, count)),
    ]


def forward_kernel(count, ahead, *refs):
    index_in, x_ref, values_in = refs[:count], refs[count], refs[count + 1 : 2 * count + 1]
    out_ref, index, values, sems, rows, blocks, even, odd = refs[2 * count + 1 + ahead :]
    copies = fetches(count, index_in, values_in, index, values, sems)
    tokens = blocks.shape[1]
    subs = blocks.shape[0] // 2
    left = left_half(tokens)
    if ahead:
        out_ref[:, 0] = refs[2 * count + 1][:, 0]
    for i in range(count):
        rows[...] = x_ref[:, i].reshape(rows.shape).astype(jnp.float32)
        for w in range(subs):
            both = rows[pl.ds(w, tokens, stride=subs), :]
            blocks[2 * w] = both.astype(jnp.bfloat16)
            blocks[2 * w + 1] = pltpu.roll(both, BLK, 1).astype(jnp.bfloat16)
        even[...] = jnp.zeros_like(even)
        odd[...] = jnp.zeros_like(odd)

        copies[2 * i].wait()
        copies[2 * i + 1].wait()

        def multiply(pair, carry):
            first, second = 2 * pair, 2 * pair + 1
            picked = [blocks[index[i, 0, n]][:, :BLK] for n in (first, second)]
            product = jnp.dot(
                jnp.concatenate(picked), values[i, pair], preferred_element_type=jnp.float32
            )
            even[index[i, 1, first]] += product[:tokens]
            odd[index[i, 1, second]] += product[tokens:]
            return carry

        lax.fori_loop(0, values.shape[1], multiply, 0, unroll=UNROLL)
        chunk = out_ref.shape[3] // LANES
        for j in range(even.shape[0] // 2):
            a, b = 2 * j, 2 * j + 1
            straight = jnp.where(left, even[a], odd[b])
            crossed = jnp.where(left, even[b], odd[a])
            summed = straight + pltpu.roll(crossed, BLK, 1)
            lanes = slice((j % chunk) * LANES, (j % chunk + 1) * LANES)
            out_ref[j // chunk, i + ahead, :, lanes] = summed.astype(jnp.bfloat16)


def forward(x, weights, n_row, ff_tile, prior=None):
    count = len(weights)
    ahead = 0 if prior is None else 1
    n_col, _, per, _ = x.shape
    tokens = n_col * PER_COL
    subs = per // PER_COL
    return pl.pallas_call(
        functools.partial(forward_kernel, count, ahead),
        out_shape=jax.ShapeDtypeStruct(
            (n_row, count + ahead, tokens, ff_tile // n_row), jnp.bfloat16
        ),
        in_specs=[ANY] * count + [VMEM] + [ANY] * count + [VMEM] * ahead,
        out_specs=VMEM,
        scratch_shapes=fetch_scratch(count, weights)
        + [
            pltpu.VMEM((n_col * per, LANES), jnp.float32),
            pltpu.VMEM((2 * subs, tokens, LANES), jnp.bfloat16),
            pltpu.VMEM((ff_tile // BLK, tokens, LANES), jnp.float32),
            pltpu.VMEM((ff_tile // BLK, tokens, LANES), jnp.float32),
        ],
        compiler_params=pltpu.CompilerParams(vmem_limit_bytes=16 * 2**20),
        cost_estimate=pl.CostEstimate(
            flops=count * 10**9, bytes_accessed=count * 2 * 2**20, transcendentals=0
        ),
    )(*[w[0] for w in weights], x, *[w[1] for w in weights], *([prior] if ahead else []))


def backward_kernel(
    index_in, hidden_ref, values_in, out_ref, index, values, sems, rows, lower, upper, total
):
    copies = fetches(1, [index_in], [values_in], index, values, sems)
    tokens = lower.shape[1]
    subs = total.shape[0] // 2
    chunk = hidden_ref.shape[2] // LANES
    left = left_half(tokens)
    for j in range(lower.shape[0] // 2):
        lanes = slice((j % chunk) * LANES, (j % chunk + 1) * LANES)
        both = hidden_ref[j // chunk, :, lanes].astype(jnp.float32)
        turned = pltpu.roll(both, BLK, 1)
        lower[2 * j] = jnp.where(left, both, 0.0).astype(jnp.bfloat16)
        upper[2 * j + 1] = jnp.where(left, 0.0, both).astype(jnp.bfloat16)
        lower[2 * j + 1] = jnp.where(left, turned, 0.0).astype(jnp.bfloat16)
        upper[2 * j] = jnp.where(left, 0.0, turned).astype(jnp.bfloat16)
    total[...] = jnp.zeros_like(total)
    for copy in copies:
        copy.wait()

    def multiply(pair, carry):
        first, second = 2 * pair, 2 * pair + 1
        picked = jnp.concatenate([lower[index[0, 1, first]], upper[index[0, 1, second]]])
        product = lax.dot_general(
            picked, values[0, pair], (((1,), (1,)), ((), ())), preferred_element_type=jnp.float32
        )
        total[index[0, 0, first]] += product[:tokens]
        total[index[0, 0, second]] += product[tokens:]
        return carry

    lax.fori_loop(0, values.shape[1], multiply, 0, unroll=UNROLL)
    for w in range(subs):
        both = jnp.concatenate([total[2 * w], total[2 * w + 1]], axis=1)
        rows[pl.ds(w, tokens, stride=subs), :] = both
    out_ref[...] = rows[...].astype(jnp.bfloat16).reshape(out_ref.shape)


def backward(hidden_grad, weights, n_col, width):
    tokens = hidden_grad.shape[1]
    ff_tile = hidden_grad.shape[0] * hidden_grad.shape[2]
    per = PER_COL * width // LANES
    return pl.pallas_call(
        backward_kernel,
        out_shape=jax.ShapeDtypeStruct((n_col, per, LANES), jnp.bfloat16),
        in_specs=[ANY, VMEM, ANY],
        out_specs=VMEM,
        scratch_shapes=fetch_scratch(1, [weights])
        + [
            pltpu.VMEM((n_col * per, LANES), jnp.float32),
            pltpu.VMEM((ff_tile // BLK, tokens, LANES), jnp.bfloat16),
            pltpu.VMEM((ff_tile // BLK, tokens, LANES), jnp.bfloat16),
            pltpu.VMEM((width // BLK, tokens, BLK), jnp.float32),
        ],
        compiler_params=pltpu.CompilerParams(vmem_limit_bytes=16 * 2**20),
        cost_estimate=pl.CostEstimate(flops=10**9, bytes_accessed=2 * 2**20, transcendentals=0),
    )(weights[0], hidden_grad, weights[1])


def gelu_slope(hidden):
    return (
        0.5 * (1.0 + lax.erf(hidden * 0.7071067811865476))
        + hidden * jnp.exp(-0.5 * hidden * hidden) * 0.3989422804014327
    )


def local(n_row, n_col, ff, x_stash, out_grad, in_values, in_index, out_values, out_index):
    section = lax.axis_index("section")
    is_last = section == 1
    width = x_stash.shape[3]
    ff_tile = ff // n_col
    per = PER_COL * width // LANES

    def exchange(v, axis):
        return lax.all_to_all(v, axis, 0, 0)

    def gather(v, axis):
        return exchange(jnp.broadcast_to(v[None], (lax.axis_size(axis),) + v.shape), axis)

    def products(x, weights, prior=None):
        return forward(x, weights, n_row, ff_tile, prior)

    def row_sums(parts):
        return jnp.sum(exchange(parts, "row").astype(jnp.float32), axis=0)

    def add(g, part):
        return (g.astype(jnp.float32) + part).astype(jnp.bfloat16)

    def col_sum(sums, w_in):
        hidden_grad = (sums[1] * gelu_slope(sums[0])).astype(jnp.bfloat16)
        part = exchange(backward(gather(hidden_grad, "row"), w_in, n_col, width), "col")
        return jnp.sum(part.astype(jnp.float32), axis=0)

    def swap(v):
        return lax.ppermute(v, "section", SWAP)

    def shard_of(v, start):
        return lax.dynamic_slice_in_dim(v, start, PER_COL, 0).reshape(per, LANES)

    in_own, out_own = in_values[0, 0, 0], out_values[0, 0, 0]
    in_at, out_at = in_index[0, 0, 0], out_index[0, 0, 0]
    places = jnp.concatenate([in_at, out_at]).astype(jnp.bfloat16)
    places = jnp.pad(places, ((0, 12), (0, 0)))
    mine = shard_of(x_stash[0, 0], PER_COL * section)
    came = swap(jnp.concatenate([shard_of(x_stash[0, 0], PER_COL - PER_COL * section), places]))
    other = came[:per]
    at_oth = came[per : per + 4].astype(jnp.int32)
    g1 = shard_of(out_grad[0], PER_COL * section)
    shards = jnp.stack([jnp.where(is_last, mine, other), g1, jnp.where(is_last, other, mine)])
    shards, in_sent, out_sent = lax.optimization_barrier((shards, in_own, out_own))
    first = gather(shards, "col")
    in_oth, out_oth = swap(in_sent), swap(out_sent)
    own = ((in_at, in_own), (out_at, out_own))
    oth = ((at_oth[:2], in_oth), (at_oth[2:], out_oth))

    def layers(w1, w0, first, g1):
        g0 = add(g1, col_sum(row_sums(products(first[:, :2], w1)), w1[0]))
        second = gather(g0[None], "col")
        hidden0 = products(first[:, 2:], w0[:1])
        return g0, col_sum(row_sums(products(second, w0[1:], hidden0)), w0[0])

    def later_core(own, oth, *rest):
        return layers(own, oth, *rest)

    def earlier_core(own, oth, *rest):
        return layers(oth, own, *rest)

    g0, part = lax.cond(is_last, later_core, earlier_core, own, oth, first, g1)
    last = add(g0, part)

    kept = jnp.where(is_last, g0, last)
    came = swap(jnp.where(is_last, last, g0))
    result = jnp.where(is_last, jnp.stack([came, kept]), jnp.stack([kept, came]))
    return result.reshape(1, 1, 2 * PER_COL, width)


def solution(mesh):
    in_specs = (
        P("section", None, "col", "row"),
        P(None, "col", "row"),
        P("section", "row", "col", None, None, None),
        P("section", "row", "col", None, None),
        P("section", "row", "col", None, None, None),
        P("section", "row", "col", None, None),
    )
    out_specs = P("section", None, "col", "row")
    body = functools.partial(local, mesh.shape["row"], mesh.shape["col"], 65536)
    return jax.shard_map(body, mesh=mesh, in_specs=in_specs, out_specs=out_specs, check_vma=False)
```

```python
import functools

import jax
import jax.numpy as jnp
from jax import lax
from jax.experimental import pallas as pl
from jax.experimental.pallas import tpu as pltpu
from jax.sharding import PartitionSpec as P

LANES = 128
BLK = 64
PER_COL = 2
SWAP = [(0, 1), (1, 0)]
UNROLL = 32
VMEM = pl.BlockSpec(memory_space=pltpu.VMEM)
ANY = pl.BlockSpec(memory_space=pl.ANY)


def left_half(rows):
    return lax.broadcasted_iota(jnp.int32, (rows, LANES), 1) < BLK


def fetches(count, index_in, values_in, index, values, sems):
    copies = [
        pltpu.make_async_copy(source, target.at[i], sems.at[k, i])
        for i in range(count)
        for k, (source, target) in enumerate([(index_in[i], index), (values_in[i], values)])
    ]
    for copy in copies:
        copy.start()
    return copies


def fetch_scratch(count, weights):
    return [
        pltpu.SMEM((count,) + weights[0][0].shape, jnp.int32),
        pltpu.VMEM((count,) + weights[0][1].shape, jnp.bfloat16),
        pltpu.SemaphoreType.DMA((2, count)),
    ]


def forward_kernel(count, ahead, *refs):
    index_in, x_ref, values_in = refs[:count], refs[count], refs[count + 1 : 2 * count + 1]
    out_ref, index, values, sems, rows, blocks, even, odd = refs[2 * count + 1 + ahead :]
    copies = fetches(count, index_in, values_in, index, values, sems)
    tokens = blocks.shape[2]
    subs = blocks.shape[1] // 2
    left = left_half(tokens)
    if ahead:
        out_ref[:, 0] = refs[2 * count + 1][:, 0]
    for i in range(count):
        rows[...] = x_ref[:, i].reshape(rows.shape).astype(jnp.float32)
        for w in range(subs):
            both = rows[pl.ds(w, tokens, stride=subs), :]
            blocks[i, 2 * w] = both.astype(jnp.bfloat16)
            blocks[i, 2 * w + 1] = pltpu.roll(both, BLK, 1).astype(jnp.bfloat16)
    for i in range(count):
        even[...] = jnp.zeros_like(even)
        odd[...] = jnp.zeros_like(odd)

        copies[2 * i].wait()
        copies[2 * i + 1].wait()

        def multiply(pair, carry):
            first, second = 2 * pair, 2 * pair + 1
            picked = [blocks[i, index[i, 0, n]][:, :BLK] for n in (first, second)]
            product = jnp.dot(
                jnp.concatenate(picked), values[i, pair], preferred_element_type=jnp.float32
            )
            even[index[i, 1, first]] += product[:tokens]
            odd[index[i, 1, second]] += product[tokens:]
            return carry

        lax.fori_loop(0, values.shape[1], multiply, 0, unroll=UNROLL)
        chunk = out_ref.shape[3] // LANES
        for j in range(even.shape[0] // 2):
            a, b = 2 * j, 2 * j + 1
            straight = jnp.where(left, even[a], odd[b])
            crossed = jnp.where(left, even[b], odd[a])
            summed = straight + pltpu.roll(crossed, BLK, 1)
            lanes = slice((j % chunk) * LANES, (j % chunk + 1) * LANES)
            out_ref[j // chunk, i + ahead, :, lanes] = summed.astype(jnp.bfloat16)


def forward(x, weights, n_row, ff_tile, prior=None):
    count = len(weights)
    ahead = 0 if prior is None else 1
    n_col, _, per, _ = x.shape
    tokens = n_col * PER_COL
    subs = per // PER_COL
    return pl.pallas_call(
        functools.partial(forward_kernel, count, ahead),
        out_shape=jax.ShapeDtypeStruct(
            (n_row, count + ahead, tokens, ff_tile // n_row), jnp.bfloat16
        ),
        in_specs=[ANY] * count + [VMEM] + [ANY] * count + [VMEM] * ahead,
        out_specs=VMEM,
        scratch_shapes=fetch_scratch(count, weights)
        + [
            pltpu.VMEM((n_col * per, LANES), jnp.float32),
            pltpu.VMEM((count, 2 * subs, tokens, LANES), jnp.bfloat16),
            pltpu.VMEM((ff_tile // BLK, tokens, LANES), jnp.float32),
            pltpu.VMEM((ff_tile // BLK, tokens, LANES), jnp.float32),
        ],
        compiler_params=pltpu.CompilerParams(vmem_limit_bytes=16 * 2**20),
        cost_estimate=pl.CostEstimate(
            flops=count * 10**9, bytes_accessed=count * 2 * 2**20, transcendentals=0
        ),
    )(*[w[0] for w in weights], x, *[w[1] for w in weights], *([prior] if ahead else []))


def backward_kernel(index_in, hidden_ref, values_in, *refs):
    out_ref, index, values, sems, rows, lower, upper, total = refs[-8:]
    copies = fetches(1, [index_in], [values_in], index, values, sems)
    tokens = lower.shape[1]
    subs = total.shape[0] // 2
    chunk = hidden_ref.shape[2] // LANES
    left = left_half(tokens)
    for j in range(lower.shape[0] // 2):
        lanes = slice((j % chunk) * LANES, (j % chunk + 1) * LANES)
        both = hidden_ref[j // chunk, :, lanes].astype(jnp.float32)
        turned = pltpu.roll(both, BLK, 1)
        lower[2 * j] = jnp.where(left, both, 0.0).astype(jnp.bfloat16)
        upper[2 * j + 1] = jnp.where(left, 0.0, both).astype(jnp.bfloat16)
        lower[2 * j + 1] = jnp.where(left, turned, 0.0).astype(jnp.bfloat16)
        upper[2 * j] = jnp.where(left, 0.0, turned).astype(jnp.bfloat16)
    total[...] = jnp.zeros_like(total)
    for copy in copies:
        copy.wait()

    def multiply(pair, carry):
        first, second = 2 * pair, 2 * pair + 1
        picked = jnp.concatenate([lower[index[0, 1, first]], upper[index[0, 1, second]]])
        product = lax.dot_general(
            picked, values[0, pair], (((1,), (1,)), ((), ())), preferred_element_type=jnp.float32
        )
        total[index[0, 0, first]] += product[:tokens]
        total[index[0, 0, second]] += product[tokens:]
        return carry

    lax.fori_loop(0, values.shape[1], multiply, 0, unroll=UNROLL)
    for w in range(subs):
        both = jnp.concatenate([total[2 * w], total[2 * w + 1]], axis=1)
        rows[pl.ds(w, tokens, stride=subs), :] = both
    n_col = out_ref.shape[0]
    per = rows.shape[0] // n_col
    out_ref[:, :per] = rows[...].astype(jnp.bfloat16).reshape(n_col, per, LANES)
    if len(refs) > 8:
        out_ref[:, per:] = jnp.broadcast_to(refs[0][...][None], (n_col,) + refs[0].shape)


def backward(hidden_grad, weights, n_col, width, more):
    tokens = hidden_grad.shape[1]
    ff_tile = hidden_grad.shape[0] * hidden_grad.shape[2]
    per = PER_COL * width // LANES
    return pl.pallas_call(
        backward_kernel,
        out_shape=jax.ShapeDtypeStruct(
            (n_col, per + sum(m.shape[0] for m in more), LANES), jnp.bfloat16
        ),
        in_specs=[ANY, VMEM, ANY] + [VMEM] * len(more),
        out_specs=VMEM,
        scratch_shapes=fetch_scratch(1, [weights])
        + [
            pltpu.VMEM((n_col * per, LANES), jnp.float32),
            pltpu.VMEM((ff_tile // BLK, tokens, LANES), jnp.bfloat16),
            pltpu.VMEM((ff_tile // BLK, tokens, LANES), jnp.bfloat16),
            pltpu.VMEM((width // BLK, tokens, BLK), jnp.float32),
        ],
        compiler_params=pltpu.CompilerParams(vmem_limit_bytes=16 * 2**20),
        cost_estimate=pl.CostEstimate(flops=10**9, bytes_accessed=2 * 2**20, transcendentals=0),
    )(weights[0], hidden_grad, weights[1], *more)


def gelu_slope(hidden):
    return (
        0.5 * (1.0 + lax.erf(hidden * 0.7071067811865476))
        + hidden * jnp.exp(-0.5 * hidden * hidden) * 0.3989422804014327
    )


def local(n_row, n_col, ff, x_stash, out_grad, in_values, in_index, out_values, out_index):
    section = lax.axis_index("section")
    is_last = section == 1
    width = x_stash.shape[3]
    ff_tile = ff // n_col
    per = PER_COL * width // LANES

    def exchange(v, axis):
        return lax.all_to_all(v, axis, 0, 0)

    def gather(v, axis):
        return exchange(jnp.broadcast_to(v[None], (lax.axis_size(axis),) + v.shape), axis)

    def products(x, weights, prior=None):
        return forward(x, weights, n_row, ff_tile, prior)

    def row_sums(parts):
        return jnp.sum(exchange(parts, "row").astype(jnp.float32), axis=0)

    def add(g, part):
        return (g.astype(jnp.float32) + part).astype(jnp.bfloat16)

    def scatter(sums, w_in, *more):
        hidden_grad = (sums[1] * gelu_slope(sums[0])).astype(jnp.bfloat16)
        return exchange(backward(gather(hidden_grad, "row"), w_in, n_col, width, more), "col")

    def total(parts):
        return jnp.sum(parts[:, :per].astype(jnp.float32), axis=0)

    def swap(v):
        return lax.ppermute(v, "section", SWAP)

    def shard_of(v, start):
        return lax.dynamic_slice_in_dim(v, start, PER_COL, 0).reshape(per, LANES)

    in_own, out_own = in_values[0, 0, 0], out_values[0, 0, 0]
    in_at, out_at = in_index[0, 0, 0], out_index[0, 0, 0]
    places = jnp.concatenate([in_at, out_at]).astype(jnp.bfloat16)
    places = jnp.pad(places, ((0, 12), (0, 0)))
    mine = shard_of(x_stash[0, 0], PER_COL * section)
    came = swap(jnp.concatenate([shard_of(x_stash[0, 0], PER_COL - PER_COL * section), places]))
    other = came[:per]
    at_oth = came[per : per + 4].astype(jnp.int32)
    g1 = shard_of(out_grad[0], PER_COL * section)
    x0 = jnp.where(is_last, other, mine)
    shards = jnp.concatenate([jnp.where(is_last, mine, other), g1, x0[: per // 2]])
    shards, in_sent, out_sent = lax.optimization_barrier((shards, in_own, out_own))
    first = gather(shards, "col")
    in_oth, out_oth = swap(in_sent), swap(out_sent)
    own = ((in_at, in_own), (out_at, out_own))
    oth = ((at_oth[:2], in_oth), (at_oth[2:], out_oth))

    def layers(w1, w0, first, g1, more):
        x1_g1 = first[:, : 2 * per].reshape(n_col, 2, per, LANES)
        parts = scatter(row_sums(products(x1_g1, w1)), w1[0], more)
        g0 = add(g1, total(parts))
        second = gather(g0[None], "col")
        x0_all = jnp.concatenate([first[:, 2 * per :], parts[:, per:]], axis=1)
        hidden0 = products(x0_all[:, None], w0[:1])
        return g0, total(scatter(row_sums(products(second, w0[1:], hidden0)), w0[0]))

    def later_core(own, oth, *rest):
        return layers(own, oth, *rest)

    def earlier_core(own, oth, *rest):
        return layers(oth, own, *rest)

    g0, part = lax.cond(is_last, later_core, earlier_core, own, oth, first, g1, x0[per // 2 :])
    last = add(g0, part)

    kept = jnp.where(is_last, g0, last)
    came = swap(jnp.where(is_last, last, g0))
    result = jnp.where(is_last, jnp.stack([came, kept]), jnp.stack([kept, came]))
    return result.reshape(1, 1, 2 * PER_COL, width)


def solution(mesh):
    in_specs = (
        P("section", None, "col", "row"),
        P(None, "col", "row"),
        P("section", "row", "col", None, None, None),
        P("section", "row", "col", None, None),
        P("section", "row", "col", None, None, None),
        P("section", "row", "col", None, None),
    )
    out_specs = P("section", None, "col", "row")
    body = functools.partial(local, mesh.shape["row"], mesh.shape["col"], 65536)
    return jax.shard_map(body, mesh=mesh, in_specs=in_specs, out_specs=out_specs, check_vma=False)
```

```python
import functools

import jax
import jax.numpy as jnp
from jax import lax
from jax.experimental import pallas as pl
from jax.experimental.pallas import tpu as pltpu
from jax.sharding import PartitionSpec as P

LANES = 128
BLK = 64
PER_COL = 2
SWAP = [(0, 1), (1, 0)]
UNROLL = 32
VMEM = pl.BlockSpec(memory_space=pltpu.VMEM)
ANY = pl.BlockSpec(memory_space=pl.ANY)


def left_half(rows):
    return lax.broadcasted_iota(jnp.int32, (rows, LANES), 1) < BLK


def fetches(count, index_in, values_in, index, values, sems):
    copies = [
        pltpu.make_async_copy(source, target.at[i], sems.at[k, i])
        for i in range(count)
        for k, (source, target) in enumerate([(index_in[i], index), (values_in[i], values)])
    ]
    for copy in copies:
        copy.start()
    return copies


def fetch_scratch(count, weights):
    return [
        pltpu.SMEM((count,) + weights[0][0].shape, jnp.int32),
        pltpu.VMEM((count,) + weights[0][1].shape, jnp.bfloat16),
        pltpu.SemaphoreType.DMA((2, count)),
    ]


def forward_kernel(count, ahead, *refs):
    index_in, x_ref, values_in = refs[:count], refs[count], refs[count + 1 : 2 * count + 1]
    out_ref, index, values, sems, rows, blocks, even, odd = refs[2 * count + 1 + ahead :]
    copies = fetches(count, index_in, values_in, index, values, sems)
    tokens = blocks.shape[2]
    subs = blocks.shape[1] // 2
    left = left_half(tokens)
    if ahead:
        out_ref[:, 0] = refs[2 * count + 1][:, 0]
    for i in range(count):
        rows[...] = x_ref[:, i].reshape(rows.shape).astype(jnp.float32)
        for w in range(subs):
            both = rows[pl.ds(w, tokens, stride=subs), :]
            blocks[i, 2 * w] = both.astype(jnp.bfloat16)
            blocks[i, 2 * w + 1] = pltpu.roll(both, BLK, 1).astype(jnp.bfloat16)
    for i in range(count):
        even[...] = jnp.zeros_like(even)
        odd[...] = jnp.zeros_like(odd)

        copies[2 * i].wait()
        copies[2 * i + 1].wait()

        def multiply(pair, carry):
            first, second = 2 * pair, 2 * pair + 1
            picked = [blocks[i, index[i, 0, n]][:, :BLK] for n in (first, second)]
            product = jnp.dot(
                jnp.concatenate(picked), values[i, pair], preferred_element_type=jnp.float32
            )
            even[index[i, 1, first]] += product[:tokens]
            odd[index[i, 1, second]] += product[tokens:]
            return carry

        lax.fori_loop(0, values.shape[1], multiply, 0, unroll=UNROLL)
        chunk = out_ref.shape[3] // LANES
        for j in range(even.shape[0] // 2):
            a, b = 2 * j, 2 * j + 1
            straight = jnp.where(left, even[a], odd[b])
            crossed = jnp.where(left, even[b], odd[a])
            summed = straight + pltpu.roll(crossed, BLK, 1)
            lanes = slice((j % chunk) * LANES, (j % chunk + 1) * LANES)
            out_ref[j // chunk, i + ahead, :, lanes] = summed.astype(jnp.bfloat16)


def forward(x, weights, n_row, ff_tile, prior=None):
    count = len(weights)
    ahead = 0 if prior is None else 1
    n_col, _, per, _ = x.shape
    tokens = n_col * PER_COL
    subs = per // PER_COL
    return pl.pallas_call(
        functools.partial(forward_kernel, count, ahead),
        out_shape=jax.ShapeDtypeStruct(
            (n_row, count + ahead, tokens, ff_tile // n_row), jnp.bfloat16
        ),
        in_specs=[ANY] * count + [VMEM] + [ANY] * count + [VMEM] * ahead,
        out_specs=VMEM,
        scratch_shapes=fetch_scratch(count, weights)
        + [
            pltpu.VMEM((n_col * per, LANES), jnp.float32),
            pltpu.VMEM((count, 2 * subs, tokens, LANES), jnp.bfloat16),
            pltpu.VMEM((ff_tile // BLK, tokens, LANES), jnp.float32),
            pltpu.VMEM((ff_tile // BLK, tokens, LANES), jnp.float32),
        ],
        compiler_params=pltpu.CompilerParams(vmem_limit_bytes=16 * 2**20),
        cost_estimate=pl.CostEstimate(
            flops=count * 10**9, bytes_accessed=count * 2 * 2**20, transcendentals=0
        ),
    )(*[w[0] for w in weights], x, *[w[1] for w in weights], *([prior] if ahead else []))


def backward_kernel(index_in, hidden_ref, values_in, *refs):
    out_ref, index, values, sems, rows, lower, upper, total = refs[-8:]
    copies = fetches(1, [index_in], [values_in], index, values, sems)
    tokens = lower.shape[1]
    subs = total.shape[0] // 2
    chunk = hidden_ref.shape[2] // LANES
    left = left_half(tokens)
    for j in range(lower.shape[0] // 2):
        lanes = slice((j % chunk) * LANES, (j % chunk + 1) * LANES)
        both = hidden_ref[j // chunk, :, lanes].astype(jnp.float32)
        turned = pltpu.roll(both, BLK, 1)
        lower[2 * j] = jnp.where(left, both, 0.0).astype(jnp.bfloat16)
        upper[2 * j + 1] = jnp.where(left, 0.0, both).astype(jnp.bfloat16)
        lower[2 * j + 1] = jnp.where(left, turned, 0.0).astype(jnp.bfloat16)
        upper[2 * j] = jnp.where(left, 0.0, turned).astype(jnp.bfloat16)
    total[...] = jnp.zeros_like(total)
    for copy in copies:
        copy.wait()

    def multiply(pair, carry):
        first, second = 2 * pair, 2 * pair + 1
        picked = jnp.concatenate([lower[index[0, 1, first]], upper[index[0, 1, second]]])
        product = lax.dot_general(
            picked, values[0, pair], (((1,), (1,)), ((), ())), preferred_element_type=jnp.float32
        )
        total[index[0, 0, first]] += product[:tokens]
        total[index[0, 0, second]] += product[tokens:]
        return carry

    lax.fori_loop(0, values.shape[1], multiply, 0, unroll=UNROLL)
    for w in range(subs):
        both = jnp.concatenate([total[2 * w], total[2 * w + 1]], axis=1)
        rows[pl.ds(w, tokens, stride=subs), :] = both
    n_col = out_ref.shape[0]
    per = rows.shape[0] // n_col
    out_ref[:, :per] = rows[...].astype(jnp.bfloat16).reshape(n_col, per, LANES)
    if len(refs) > 8:
        out_ref[:, per:] = jnp.broadcast_to(refs[0][...][None], (n_col,) + refs[0].shape)


def backward(hidden_grad, weights, n_col, width, more):
    tokens = hidden_grad.shape[1]
    ff_tile = hidden_grad.shape[0] * hidden_grad.shape[2]
    per = PER_COL * width // LANES
    return pl.pallas_call(
        backward_kernel,
        out_shape=jax.ShapeDtypeStruct(
            (n_col, per + sum(m.shape[0] for m in more), LANES), jnp.bfloat16
        ),
        in_specs=[ANY, VMEM, ANY] + [VMEM] * len(more),
        out_specs=VMEM,
        scratch_shapes=fetch_scratch(1, [weights])
        + [
            pltpu.VMEM((n_col * per, LANES), jnp.float32),
            pltpu.VMEM((ff_tile // BLK, tokens, LANES), jnp.bfloat16),
            pltpu.VMEM((ff_tile // BLK, tokens, LANES), jnp.bfloat16),
            pltpu.VMEM((width // BLK, tokens, BLK), jnp.float32),
        ],
        compiler_params=pltpu.CompilerParams(vmem_limit_bytes=16 * 2**20),
        cost_estimate=pl.CostEstimate(flops=10**9, bytes_accessed=2 * 2**20, transcendentals=0),
    )(weights[0], hidden_grad, weights[1], *more)


def gelu_slope(hidden):
    return (
        0.5 * (1.0 + lax.erf(hidden * 0.7071067811865476))
        + hidden * jnp.exp(-0.5 * hidden * hidden) * 0.3989422804014327
    )


def local(n_row, n_col, ff, x_stash, out_grad, in_values, in_index, out_values, out_index):
    section = lax.axis_index("section")
    is_last = section == 1
    width = x_stash.shape[3]
    ff_tile = ff // n_col
    per = PER_COL * width // LANES

    def exchange(v, axis):
        return lax.all_to_all(v, axis, 0, 0)

    def gather(v, axis):
        return exchange(jnp.broadcast_to(v[None], (lax.axis_size(axis),) + v.shape), axis)

    def products(x, weights, prior=None):
        return forward(x, weights, n_row, ff_tile, prior)

    def row_sums(parts):
        return jnp.sum(exchange(parts, "row").astype(jnp.float32), axis=0)

    def add(g, part):
        return (g.astype(jnp.float32) + part).astype(jnp.bfloat16)

    def scatter(sums, w_in, *more):
        hidden_grad = (sums[1] * gelu_slope(sums[0])).astype(jnp.bfloat16)
        return exchange(backward(gather(hidden_grad, "row"), w_in, n_col, width, more), "col")

    def total(parts):
        return jnp.sum(parts[:, :per].astype(jnp.float32), axis=0)

    def swap(v):
        return lax.ppermute(v, "section", SWAP)

    def shard_of(v, start):
        return lax.dynamic_slice_in_dim(v, start, PER_COL, 0).reshape(per, LANES)

    in_own, out_own = in_values[0, 0, 0], out_values[0, 0, 0]
    in_at, out_at = in_index[0, 0, 0], out_index[0, 0, 0]
    places = jnp.concatenate([in_at, out_at]).astype(jnp.bfloat16)
    places = jnp.pad(places, ((0, 12), (0, 0)))
    mine = shard_of(x_stash[0, 0], PER_COL * section)
    came = swap(jnp.concatenate([shard_of(x_stash[0, 0], PER_COL - PER_COL * section), places]))
    other = came[:per]
    at_oth = came[per : per + 4].astype(jnp.int32)
    g1 = shard_of(out_grad[0], PER_COL * section)
    x0 = jnp.where(is_last, other, mine)
    shards = jnp.stack([jnp.where(is_last, mine, other), g1])
    shards, in_sent, out_sent = lax.optimization_barrier((shards, in_own, out_own))
    first = gather(shards, "col")
    in_oth, out_oth = swap(in_sent), swap(out_sent)
    own = ((in_at, in_own), (out_at, out_own))
    oth = ((at_oth[:2], in_oth), (at_oth[2:], out_oth))

    def later_core(own, oth, first, g1, x0):
        w1, w0 = own, oth
        g0 = add(g1, total(scatter(row_sums(products(first, w1)), w1[0])))
        second = gather(jnp.stack([x0, g0]), "col")
        return g0, total(scatter(row_sums(products(second, w0)), w0[0]))

    def earlier_core(own, oth, first, g1, x0):
        w1, w0 = oth, own
        parts = scatter(row_sums(products(first, w1)), w1[0], x0)
        g0 = add(g1, total(parts))
        second = gather(g0[None], "col")
        hidden0 = products(parts[:, None, per:], w0[:1])
        return g0, total(scatter(row_sums(products(second, w0[1:], hidden0)), w0[0]))

    g0, part = lax.cond(is_last, later_core, earlier_core, own, oth, first, g1, x0)
    last = add(g0, part)

    kept = jnp.where(is_last, g0, last)
    came = swap(jnp.where(is_last, last, g0))
    result = jnp.where(is_last, jnp.stack([came, kept]), jnp.stack([kept, came]))
    return result.reshape(1, 1, 2 * PER_COL, width)


def solution(mesh):
    in_specs = (
        P("section", None, "col", "row"),
        P(None, "col", "row"),
        P("section", "row", "col", None, None, None),
        P("section", "row", "col", None, None),
        P("section", "row", "col", None, None, None),
        P("section", "row", "col", None, None),
    )
    out_specs = P("section", None, "col", "row")
    body = functools.partial(local, mesh.shape["row"], mesh.shape["col"], 65536)
    return jax.shard_map(body, mesh=mesh, in_specs=in_specs, out_specs=out_specs, check_vma=False)
```

```python
import functools

import jax
import jax.numpy as jnp
from jax import lax
from jax.experimental import pallas as pl
from jax.experimental.pallas import tpu as pltpu
from jax.sharding import PartitionSpec as P

LANES = 128
BLK = 64
PER_COL = 2
SWAP = [(0, 1), (1, 0)]
UNROLL = 32
VMEM = pl.BlockSpec(memory_space=pltpu.VMEM)
ANY = pl.BlockSpec(memory_space=pl.ANY)


def left_half(rows):
    return lax.broadcasted_iota(jnp.int32, (rows, LANES), 1) < BLK


def fetches(count, index_in, values_in, index, values, sems):
    copies = [
        pltpu.make_async_copy(source, target.at[i], sems.at[k, i])
        for i in range(count)
        for k, (source, target) in enumerate([(index_in[i], index), (values_in[i], values)])
    ]
    for copy in copies:
        copy.start()
    return copies


def fetch_scratch(count, weights):
    return [
        pltpu.SMEM((count,) + weights[0][0].shape, jnp.int32),
        pltpu.VMEM((count,) + weights[0][1].shape, jnp.bfloat16),
        pltpu.SemaphoreType.DMA((2, count)),
    ]


def forward_kernel(count, ahead, *refs):
    index_in, x_ref, values_in = refs[:count], refs[count], refs[count + 1 : 2 * count + 1]
    out_ref, index, values, sems, rows, blocks, even, odd = refs[2 * count + 1 + ahead :]
    copies = fetches(count, index_in, values_in, index, values, sems)
    tokens = blocks.shape[2]
    subs = blocks.shape[1] // 2
    left = left_half(tokens)
    if ahead:
        out_ref[:, 0] = refs[2 * count + 1][:, 0]
    for i in range(count):
        rows[...] = x_ref[:, i].reshape(rows.shape).astype(jnp.float32)
        for w in range(subs):
            both = rows[pl.ds(w, tokens, stride=subs), :]
            blocks[i, 2 * w] = both.astype(jnp.bfloat16)
            blocks[i, 2 * w + 1] = pltpu.roll(both, BLK, 1).astype(jnp.bfloat16)
    for i in range(count):
        even[...] = jnp.zeros_like(even)
        odd[...] = jnp.zeros_like(odd)

        copies[2 * i].wait()
        copies[2 * i + 1].wait()

        def multiply(pair, carry):
            first, second = 2 * pair, 2 * pair + 1
            picked = [blocks[i, index[i, 0, n]][:, :BLK] for n in (first, second)]
            product = jnp.dot(
                jnp.concatenate(picked), values[i, pair], preferred_element_type=jnp.float32
            )
            even[index[i, 1, first]] += product[:tokens]
            odd[index[i, 1, second]] += product[tokens:]
            return carry

        lax.fori_loop(0, values.shape[1], multiply, 0, unroll=UNROLL)
        chunk = out_ref.shape[3] // LANES
        for j in range(even.shape[0] // 2):
            a, b = 2 * j, 2 * j + 1
            straight = jnp.where(left, even[a], odd[b])
            crossed = jnp.where(left, even[b], odd[a])
            summed = straight + pltpu.roll(crossed, BLK, 1)
            lanes = slice((j % chunk) * LANES, (j % chunk + 1) * LANES)
            out_ref[j // chunk, i + ahead, :, lanes] = summed.astype(jnp.bfloat16)


def forward(x, weights, n_row, ff_tile, prior=None):
    count = len(weights)
    ahead = 0 if prior is None else 1
    n_col, _, per, _ = x.shape
    tokens = n_col * PER_COL
    subs = per // PER_COL
    return pl.pallas_call(
        functools.partial(forward_kernel, count, ahead),
        out_shape=jax.ShapeDtypeStruct(
            (n_row, count + ahead, tokens, ff_tile // n_row), jnp.bfloat16
        ),
        in_specs=[ANY] * count + [VMEM] + [ANY] * count + [VMEM] * ahead,
        out_specs=VMEM,
        scratch_shapes=fetch_scratch(count, weights)
        + [
            pltpu.VMEM((n_col * per, LANES), jnp.float32),
            pltpu.VMEM((count, 2 * subs, tokens, LANES), jnp.bfloat16),
            pltpu.VMEM((ff_tile // BLK, tokens, LANES), jnp.float32),
            pltpu.VMEM((ff_tile // BLK, tokens, LANES), jnp.float32),
        ],
        compiler_params=pltpu.CompilerParams(vmem_limit_bytes=16 * 2**20),
        cost_estimate=pl.CostEstimate(
            flops=count * 10**9, bytes_accessed=count * 2 * 2**20, transcendentals=0
        ),
    )(*[w[0] for w in weights], x, *[w[1] for w in weights], *([prior] if ahead else []))


def backward_kernel(index_in, hidden_ref, values_in, *refs):
    out_ref, index, values, sems, rows, lower, upper, total = refs[-8:]
    copies = fetches(1, [index_in], [values_in], index, values, sems)
    tokens = lower.shape[1]
    subs = total.shape[0] // 2
    chunk = hidden_ref.shape[2] // LANES
    left = left_half(tokens)
    for j in range(lower.shape[0] // 2):
        lanes = slice((j % chunk) * LANES, (j % chunk + 1) * LANES)
        both = hidden_ref[j // chunk, :, lanes].astype(jnp.float32)
        turned = pltpu.roll(both, BLK, 1)
        lower[2 * j] = jnp.where(left, both, 0.0).astype(jnp.bfloat16)
        upper[2 * j + 1] = jnp.where(left, 0.0, both).astype(jnp.bfloat16)
        lower[2 * j + 1] = jnp.where(left, turned, 0.0).astype(jnp.bfloat16)
        upper[2 * j] = jnp.where(left, 0.0, turned).astype(jnp.bfloat16)
    total[...] = jnp.zeros_like(total)
    for copy in copies:
        copy.wait()

    def multiply(pair, carry):
        first, second = 2 * pair, 2 * pair + 1
        picked = jnp.concatenate([lower[index[0, 1, first]], upper[index[0, 1, second]]])
        product = lax.dot_general(
            picked, values[0, pair], (((1,), (1,)), ((), ())), preferred_element_type=jnp.float32
        )
        total[index[0, 0, first]] += product[:tokens]
        total[index[0, 0, second]] += product[tokens:]
        return carry

    lax.fori_loop(0, values.shape[1], multiply, 0, unroll=UNROLL)
    for w in range(subs):
        both = jnp.concatenate([total[2 * w], total[2 * w + 1]], axis=1)
        rows[pl.ds(w, tokens, stride=subs), :] = both
    n_col = out_ref.shape[0]
    per = rows.shape[0] // n_col
    out_ref[:, :per] = rows[...].astype(jnp.bfloat16).reshape(n_col, per, LANES)
    if len(refs) > 8:
        out_ref[:, per:] = jnp.broadcast_to(refs[0][...][None], (n_col,) + refs[0].shape)


def backward(hidden_grad, weights, n_col, width, more):
    tokens = hidden_grad.shape[1]
    ff_tile = hidden_grad.shape[0] * hidden_grad.shape[2]
    per = PER_COL * width // LANES
    return pl.pallas_call(
        backward_kernel,
        out_shape=jax.ShapeDtypeStruct(
            (n_col, per + sum(m.shape[0] for m in more), LANES), jnp.bfloat16
        ),
        in_specs=[ANY, VMEM, ANY] + [VMEM] * len(more),
        out_specs=VMEM,
        scratch_shapes=fetch_scratch(1, [weights])
        + [
            pltpu.VMEM((n_col * per, LANES), jnp.float32),
            pltpu.VMEM((ff_tile // BLK, tokens, LANES), jnp.bfloat16),
            pltpu.VMEM((ff_tile // BLK, tokens, LANES), jnp.bfloat16),
            pltpu.VMEM((width // BLK, tokens, BLK), jnp.float32),
        ],
        compiler_params=pltpu.CompilerParams(vmem_limit_bytes=16 * 2**20),
        cost_estimate=pl.CostEstimate(flops=10**9, bytes_accessed=2 * 2**20, transcendentals=0),
    )(weights[0], hidden_grad, weights[1], *more)


def gelu_slope(hidden):
    return (
        0.5 * (1.0 + lax.erf(hidden * 0.7071067811865476))
        + hidden * jnp.exp(-0.5 * hidden * hidden) * 0.3989422804014327
    )


def local(n_row, n_col, ff, x_stash, out_grad, in_values, in_index, out_values, out_index):
    section = lax.axis_index("section")
    is_last = section == 1
    width = x_stash.shape[3]
    ff_tile = ff // n_col
    per = PER_COL * width // LANES

    def exchange(v, axis):
        return lax.all_to_all(v, axis, 0, 0)

    def gather(v, axis):
        return exchange(jnp.broadcast_to(v[None], (lax.axis_size(axis),) + v.shape), axis)

    def products(x, weights, prior=None):
        return forward(x, weights, n_row, ff_tile, prior)

    def row_sums(parts):
        return jnp.sum(exchange(parts, "row").astype(jnp.float32), axis=0)

    def add(g, part):
        return (g.astype(jnp.float32) + part).astype(jnp.bfloat16)

    def scatter(sums, w_in, *more):
        hidden_grad = (sums[1] * gelu_slope(sums[0])).astype(jnp.bfloat16)
        return exchange(backward(gather(hidden_grad, "row"), w_in, n_col, width, more), "col")

    def total(parts):
        return jnp.sum(parts[:, :per].astype(jnp.float32), axis=0)

    def swap(v):
        return lax.ppermute(v, "section", SWAP)

    def shard_of(v, start):
        return lax.dynamic_slice_in_dim(v, start, PER_COL, 0).reshape(per, LANES)

    in_own, out_own = in_values[0, 0, 0], out_values[0, 0, 0]
    in_at, out_at = in_index[0, 0, 0], out_index[0, 0, 0]
    places = jnp.concatenate([in_at, out_at]).astype(jnp.bfloat16)
    places = jnp.pad(places, ((0, 12), (0, 0)))
    mine = shard_of(x_stash[0, 0], PER_COL * section)
    came = swap(jnp.concatenate([shard_of(x_stash[0, 0], PER_COL - PER_COL * section), places]))
    other = came[:per]
    at_oth = came[per : per + 4].astype(jnp.int32)
    g1 = shard_of(out_grad[0], PER_COL * section)
    x0 = jnp.where(is_last, other, mine)
    shards = jnp.concatenate([jnp.where(is_last, mine, other), g1, x0[: per // 2]])
    shards, in_sent, out_sent = lax.optimization_barrier((shards, in_own, out_own))
    first = gather(shards, "col")
    in_oth, out_oth = swap(in_sent), swap(out_sent)
    own = ((in_at, in_own), (out_at, out_own))
    oth = ((at_oth[:2], in_oth), (at_oth[2:], out_oth))

    def both_of(first):
        return first[:, : 2 * per].reshape(n_col, 2, per, LANES)

    def later_core(own, oth, first, g1, more):
        w1, w0 = own, oth
        g0 = add(g1, total(scatter(row_sums(products(both_of(first), w1)), w1[0])))
        second = gather(jnp.concatenate([g0, more]), "col")
        x0_all = jnp.concatenate([first[:, 2 * per :], second[:, per:]], axis=1)
        x0_g0 = jnp.stack([x0_all, second[:, :per]], axis=1)
        return g0, total(scatter(row_sums(products(x0_g0, w0)), w0[0]))

    def earlier_core(own, oth, first, g1, more):
        w1, w0 = oth, own
        parts = scatter(row_sums(products(both_of(first), w1)), w1[0], more)
        g0 = add(g1, total(parts))
        second = gather(g0[None], "col")
        x0_all = jnp.concatenate([first[:, 2 * per :], parts[:, per:]], axis=1)
        hidden0 = products(x0_all[:, None], w0[:1])
        return g0, total(scatter(row_sums(products(second, w0[1:], hidden0)), w0[0]))

    g0, part = lax.cond(is_last, later_core, earlier_core, own, oth, first, g1, x0[per // 2 :])
    last = add(g0, part)

    kept = jnp.where(is_last, g0, last)
    came = swap(jnp.where(is_last, last, g0))
    result = jnp.where(is_last, jnp.stack([came, kept]), jnp.stack([kept, came]))
    return result.reshape(1, 1, 2 * PER_COL, width)


def solution(mesh):
    in_specs = (
        P("section", None, "col", "row"),
        P(None, "col", "row"),
        P("section", "row", "col", None, None, None),
        P("section", "row", "col", None, None),
        P("section", "row", "col", None, None, None),
        P("section", "row", "col", None, None),
    )
    out_specs = P("section", None, "col", "row")
    body = functools.partial(local, mesh.shape["row"], mesh.shape["col"], 65536)
    return jax.shard_map(body, mesh=mesh, in_specs=in_specs, out_specs=out_specs, check_vma=False)
```

```python
import functools

import jax
import jax.numpy as jnp
from jax import lax
from jax.experimental import pallas as pl
from jax.experimental.pallas import tpu as pltpu
from jax.sharding import PartitionSpec as P

LANES = 128
BLK = 64
PER_COL = 2
SWAP = [(0, 1), (1, 0)]
UNROLL = 64
VMEM = pl.BlockSpec(memory_space=pltpu.VMEM)
ANY = pl.BlockSpec(memory_space=pl.ANY)


def left_half(rows):
    return lax.broadcasted_iota(jnp.int32, (rows, LANES), 1) < BLK


def fetches(count, index_in, values_in, index, values, sems):
    copies = [
        pltpu.make_async_copy(source, target.at[i], sems.at[k, i])
        for i in range(count)
        for k, (source, target) in enumerate([(index_in[i], index), (values_in[i], values)])
    ]
    for copy in copies:
        copy.start()
    return copies


def fetch_scratch(count, weights):
    return [
        pltpu.SMEM((count,) + weights[0][0].shape, jnp.int32),
        pltpu.VMEM((count,) + weights[0][1].shape, jnp.bfloat16),
        pltpu.SemaphoreType.DMA((2, count)),
    ]


def forward_kernel(count, ahead, *refs):
    index_in, x_ref, values_in = refs[:count], refs[count], refs[count + 1 : 2 * count + 1]
    out_ref, index, values, sems, rows, blocks, even, odd = refs[2 * count + 1 + ahead :]
    copies = fetches(count, index_in, values_in, index, values, sems)
    tokens = blocks.shape[2]
    subs = blocks.shape[1] // 2
    left = left_half(tokens)
    if ahead:
        out_ref[:, 0] = refs[2 * count + 1][:, 0]
    for i in range(count):
        rows[...] = x_ref[:, i].reshape(rows.shape).astype(jnp.float32)
        for w in range(subs):
            both = rows[pl.ds(w, tokens, stride=subs), :]
            blocks[i, 2 * w] = both.astype(jnp.bfloat16)
            blocks[i, 2 * w + 1] = pltpu.roll(both, BLK, 1).astype(jnp.bfloat16)
    for i in range(count):
        even[...] = jnp.zeros_like(even)
        odd[...] = jnp.zeros_like(odd)

        copies[2 * i].wait()
        copies[2 * i + 1].wait()

        def multiply(pair, carry):
            first, second = 2 * pair, 2 * pair + 1
            picked = [blocks[i, index[i, 0, n]][:, :BLK] for n in (first, second)]
            product = jnp.dot(
                jnp.concatenate(picked), values[i, pair], preferred_element_type=jnp.float32
            )
            even[index[i, 1, first]] += product[:tokens]
            odd[index[i, 1, second]] += product[tokens:]
            return carry

        lax.fori_loop(0, values.shape[1], multiply, 0, unroll=UNROLL)
        chunk = out_ref.shape[3] // LANES
        for j in range(even.shape[0] // 2):
            a, b = 2 * j, 2 * j + 1
            straight = jnp.where(left, even[a], odd[b])
            crossed = jnp.where(left, even[b], odd[a])
            summed = straight + pltpu.roll(crossed, BLK, 1)
            lanes = slice((j % chunk) * LANES, (j % chunk + 1) * LANES)
            out_ref[j // chunk, i + ahead, :, lanes] = summed.astype(jnp.bfloat16)


def forward(x, weights, n_row, ff_tile, prior=None):
    count = len(weights)
    ahead = 0 if prior is None else 1
    n_col, _, per, _ = x.shape
    tokens = n_col * PER_COL
    subs = per // PER_COL
    return pl.pallas_call(
        functools.partial(forward_kernel, count, ahead),
        out_shape=jax.ShapeDtypeStruct(
            (n_row, count + ahead, tokens, ff_tile // n_row), jnp.bfloat16
        ),
        in_specs=[ANY] * count + [VMEM] + [ANY] * count + [VMEM] * ahead,
        out_specs=VMEM,
        scratch_shapes=fetch_scratch(count, weights)
        + [
            pltpu.VMEM((n_col * per, LANES), jnp.float32),
            pltpu.VMEM((count, 2 * subs, tokens, LANES), jnp.bfloat16),
            pltpu.VMEM((ff_tile // BLK, tokens, LANES), jnp.float32),
            pltpu.VMEM((ff_tile // BLK, tokens, LANES), jnp.float32),
        ],
        compiler_params=pltpu.CompilerParams(vmem_limit_bytes=16 * 2**20),
        cost_estimate=pl.CostEstimate(
            flops=count * 10**9, bytes_accessed=count * 2 * 2**20, transcendentals=0
        ),
    )(*[w[0] for w in weights], x, *[w[1] for w in weights], *([prior] if ahead else []))


def backward_kernel(index_in, hidden_ref, values_in, *refs):
    out_ref, index, values, sems, rows, lower, upper, total = refs[-8:]
    copies = fetches(1, [index_in], [values_in], index, values, sems)
    tokens = lower.shape[1]
    subs = total.shape[0] // 2
    chunk = hidden_ref.shape[2] // LANES
    left = left_half(tokens)
    for j in range(lower.shape[0] // 2):
        lanes = slice((j % chunk) * LANES, (j % chunk + 1) * LANES)
        both = hidden_ref[j // chunk, :, lanes].astype(jnp.float32)
        turned = pltpu.roll(both, BLK, 1)
        lower[2 * j] = jnp.where(left, both, 0.0).astype(jnp.bfloat16)
        upper[2 * j + 1] = jnp.where(left, 0.0, both).astype(jnp.bfloat16)
        lower[2 * j + 1] = jnp.where(left, turned, 0.0).astype(jnp.bfloat16)
        upper[2 * j] = jnp.where(left, 0.0, turned).astype(jnp.bfloat16)
    total[...] = jnp.zeros_like(total)
    for copy in copies:
        copy.wait()

    def multiply(pair, carry):
        first, second = 2 * pair, 2 * pair + 1
        picked = jnp.concatenate([lower[index[0, 1, first]], upper[index[0, 1, second]]])
        product = lax.dot_general(
            picked, values[0, pair], (((1,), (1,)), ((), ())), preferred_element_type=jnp.float32
        )
        total[index[0, 0, first]] += product[:tokens]
        total[index[0, 0, second]] += product[tokens:]
        return carry

    lax.fori_loop(0, values.shape[1], multiply, 0, unroll=UNROLL)
    for w in range(subs):
        both = jnp.concatenate([total[2 * w], total[2 * w + 1]], axis=1)
        rows[pl.ds(w, tokens, stride=subs), :] = both
    n_col = out_ref.shape[0]
    per = rows.shape[0] // n_col
    out_ref[:, :per] = rows[...].astype(jnp.bfloat16).reshape(n_col, per, LANES)
    if len(refs) > 8:
        out_ref[:, per:] = jnp.broadcast_to(refs[0][...][None], (n_col,) + refs[0].shape)


def backward(hidden_grad, weights, n_col, width, more):
    tokens = hidden_grad.shape[1]
    ff_tile = hidden_grad.shape[0] * hidden_grad.shape[2]
    per = PER_COL * width // LANES
    return pl.pallas_call(
        backward_kernel,
        out_shape=jax.ShapeDtypeStruct(
            (n_col, per + sum(m.shape[0] for m in more), LANES), jnp.bfloat16
        ),
        in_specs=[ANY, VMEM, ANY] + [VMEM] * len(more),
        out_specs=VMEM,
        scratch_shapes=fetch_scratch(1, [weights])
        + [
            pltpu.VMEM((n_col * per, LANES), jnp.float32),
            pltpu.VMEM((ff_tile // BLK, tokens, LANES), jnp.bfloat16),
            pltpu.VMEM((ff_tile // BLK, tokens, LANES), jnp.bfloat16),
            pltpu.VMEM((width // BLK, tokens, BLK), jnp.float32),
        ],
        compiler_params=pltpu.CompilerParams(vmem_limit_bytes=16 * 2**20),
        cost_estimate=pl.CostEstimate(flops=10**9, bytes_accessed=2 * 2**20, transcendentals=0),
    )(weights[0], hidden_grad, weights[1], *more)


def gelu_slope(hidden):
    return (
        0.5 * (1.0 + lax.erf(hidden * 0.7071067811865476))
        + hidden * jnp.exp(-0.5 * hidden * hidden) * 0.3989422804014327
    )


def local(n_row, n_col, ff, x_stash, out_grad, in_values, in_index, out_values, out_index):
    section = lax.axis_index("section")
    is_last = section == 1
    width = x_stash.shape[3]
    ff_tile = ff // n_col
    per = PER_COL * width // LANES

    def exchange(v, axis):
        return lax.all_to_all(v, axis, 0, 0)

    def gather(v, axis):
        return exchange(jnp.broadcast_to(v[None], (lax.axis_size(axis),) + v.shape), axis)

    def products(x, weights, prior=None):
        return forward(x, weights, n_row, ff_tile, prior)

    def row_sums(parts):
        return jnp.sum(exchange(parts, "row").astype(jnp.float32), axis=0)

    def add(g, part):
        return (g.astype(jnp.float32) + part).astype(jnp.bfloat16)

    def scatter(sums, w_in, *more):
        hidden_grad = (sums[1] * gelu_slope(sums[0])).astype(jnp.bfloat16)
        return exchange(backward(gather(hidden_grad, "row"), w_in, n_col, width, more), "col")

    def total(parts):
        return jnp.sum(parts[:, :per].astype(jnp.float32), axis=0)

    def swap(v):
        return lax.ppermute(v, "section", SWAP)

    def shard_of(v, start):
        return lax.dynamic_slice_in_dim(v, start, PER_COL, 0).reshape(per, LANES)

    in_own, out_own = in_values[0, 0, 0], out_values[0, 0, 0]
    in_at, out_at = in_index[0, 0, 0], out_index[0, 0, 0]
    places = jnp.concatenate([in_at, out_at]).astype(jnp.bfloat16)
    places = jnp.pad(places, ((0, 12), (0, 0)))
    mine = shard_of(x_stash[0, 0], PER_COL * section)
    came = swap(jnp.concatenate([shard_of(x_stash[0, 0], PER_COL - PER_COL * section), places]))
    other = came[:per]
    at_oth = came[per : per + 4].astype(jnp.int32)
    g1 = shard_of(out_grad[0], PER_COL * section)
    x0 = jnp.where(is_last, other, mine)
    shards = jnp.concatenate([jnp.where(is_last, mine, other), g1, x0[: per // 2]])
    shards, in_sent, out_sent = lax.optimization_barrier((shards, in_own, out_own))
    first = gather(shards, "col")
    in_oth, out_oth = swap(in_sent), swap(out_sent)
    own = ((in_at, in_own), (out_at, out_own))
    oth = ((at_oth[:2], in_oth), (at_oth[2:], out_oth))

    def layers(w1, w0, first, g1, more):
        x1_g1 = first[:, : 2 * per].reshape(n_col, 2, per, LANES)
        parts = scatter(row_sums(products(x1_g1, w1)), w1[0], more)
        g0 = add(g1, total(parts))
        second = gather(g0[None], "col")
        x0_all = jnp.concatenate([first[:, 2 * per :], parts[:, per:]], axis=1)
        hidden0 = products(x0_all[:, None], w0[:1])
        return g0, total(scatter(row_sums(products(second, w0[1:], hidden0)), w0[0]))

    def later_core(own, oth, *rest):
        return layers(own, oth, *rest)

    def earlier_core(own, oth, *rest):
        return layers(oth, own, *rest)

    g0, part = lax.cond(is_last, later_core, earlier_core, own, oth, first, g1, x0[per // 2 :])
    last = add(g0, part)

    kept = jnp.where(is_last, g0, last)
    came = swap(jnp.where(is_last, last, g0))
    result = jnp.where(is_last, jnp.stack([came, kept]), jnp.stack([kept, came]))
    return result.reshape(1, 1, 2 * PER_COL, width)


def solution(mesh):
    in_specs = (
        P("section", None, "col", "row"),
        P(None, "col", "row"),
        P("section", "row", "col", None, None, None),
        P("section", "row", "col", None, None),
        P("section", "row", "col", None, None, None),
        P("section", "row", "col", None, None),
    )
    out_specs = P("section", None, "col", "row")
    body = functools.partial(local, mesh.shape["row"], mesh.shape["col"], 65536)
    return jax.shard_map(body, mesh=mesh, in_specs=in_specs, out_specs=out_specs, check_vma=False)
```
